128 devices in a mesh: row: 8 (over z, x_hi), col: 16 (over x_lo, y, core).
Axes of the slice: x: 4 (x_hi: 2, x_lo: 2; x = x_hi * 2 + x_lo), y: 4, z: 4, core: 2. Of those that a mesh axis runs over, the one named last changes fastest.
Arguments:
- acts: bfloat16 [768, 8192], P('row', 'col'), may hold values from -6 to 6
- logits: float32 [768, 2048], P('row'), may hold values from -10 to 10
- label_ids: int32 [768, 8], P('row'), may hold values from 0 to 2047
- head_weight: bfloat16 [2048, 8192], P(None, 'col'), may hold values from -0.125 to 0.125
- gate_weight: bfloat16 [8192, 28672], P('col', 'row'), may hold values from -0.0625 to 0.0625
- up_weight: bfloat16 [8192, 28672], P('col', 'row'), may hold values from -0.0625 to 0.0625
- down_weight: bfloat16 [28672, 8192], P('row', 'col'), may hold values from -0.03125 to 0.03125
Outputs:
- acts_grad: bfloat16 [768, 8192], P('row', 'col')
- gate_grad: bfloat16 [8192, 28672], P('col', 'row')
- up_grad: bfloat16 [8192, 28672], P('col', 'row')
- down_grad: bfloat16 [28672, 8192], P('row', 'col')
The draws below stay inside these ranges and needn't reach their ends.
Inputs may be any that keep to these rules, and one draw needn't show every extreme that they name: `label_ids`: a token may name a code more than once; it counts once.
All inputs are finite; a program needn't handle non-finite values.
Results may differ from the reference program's by a relative error of at most 0.035.
Values may be sent and summed in bfloat16 or wider, within the bound.
A program may use at most 192 MiB of HBM per device.

```python
import jax
import jax.numpy as jnp
from jax import lax

D = 8192
FF = 28672
CODES = 2048
LABELS = 8
TOKENS = 768
FEAT_BLOCK = 512
N_COL = 16


def touch_ends(values, stream_key, low, largest):
    spot = [jax.random.randint(jax.random.fold_in(stream_key, axis), (), 0, length) for axis, length in enumerate(values.shape)]
    main_axis = values.shape.index(max(values.shape))
    beside = spot[:main_axis] + [(spot[main_axis] + 1) % values.shape[main_axis]] + spot[main_axis + 1:]
    return values.at[tuple(spot)].set(low).at[tuple(beside)].set(largest)


def shard_levels(rng, extent, cuts, smallest, top_value):
    level, own = 1.0, jax.random.fold_in(rng, 6)
    for axis_at, shards_of in cuts:
        draws = jnp.exp(jax.random.uniform(jax.random.fold_in(own, axis_at), (shards_of,), jnp.float32, smallest / len(cuts), top_value / len(cuts)))
        level = level * jnp.repeat(draws, extent[axis_at] // shards_of).reshape([-1 if axis == axis_at else 1 for axis in range(len(extent))])
    return level


def normal_values(stream_key, shape, width, reach, split=(), held_as=jnp.bfloat16):
    loudness = shard_levels(stream_key, shape, split, -0.22, 0.18) if split else 1.0
    result = jax.random.normal(stream_key, shape, jnp.float32) * width * loudness
    return jnp.minimum(jnp.maximum(result, -reach), reach).astype(held_as)


def setup_inputs(seed: int = 0) -> dict:
    arg_keys = jax.random.split(jax.random.key(seed), 8)
    return {
        "acts": normal_values(arg_keys[0], (TOKENS, D), 1.0, 6.0, ((0, 8), (1, 16))),
        "logits": normal_values(arg_keys[1], (TOKENS, CODES), 2.0, 10.0, ((0, 8),), jnp.float32),
        "label_ids": touch_ends(jax.random.randint(arg_keys[2], (TOKENS, LABELS), 0, CODES), jax.random.fold_in(arg_keys[2], 1), 0, CODES - 1).astype(jnp.int32),
        "head_weight": normal_values(arg_keys[3], (CODES, D), CODES ** -0.5, 0.125, ((1, 16),)),
        "gate_weight": normal_values(arg_keys[4], (D, FF), D ** -0.5, 0.0625, ((0, 16), (1, 8))),
        "up_weight": normal_values(arg_keys[5], (D, FF), D ** -0.5, 0.0625, ((0, 16), (1, 8))),
        "down_weight": normal_values(arg_keys[6], (FF, D), FF ** -0.5, 0.03125, ((0, 8), (1, 16))),
    }


def reference(acts, logits, label_ids, head_weight, gate_weight, up_weight, down_weight):
    codes = lax.broadcasted_iota(jnp.int32, (1, 1, CODES), 2)
    target = jnp.max((label_ids[:, :, None] == codes).astype(jnp.float32), axis=1)
    logit_grad = (jax.nn.sigmoid(logits) - target).astype(jnp.bfloat16)
    out_grad = jnp.dot(logit_grad, head_weight, preferred_element_type=jnp.float32).astype(jnp.bfloat16)
    trans_dims = (((1,), (1,)), ((), ()))

    def block_step(carry, index):
        start = index * FEAT_BLOCK
        rows_x = lax.dynamic_slice_in_dim(acts, start, FEAT_BLOCK, 1)
        rows_g = lax.dynamic_slice_in_dim(out_grad, start, FEAT_BLOCK, 1)
        part_g = lax.dynamic_slice_in_dim(gate_weight, start, FEAT_BLOCK, 0)
        part_u = lax.dynamic_slice_in_dim(up_weight, start, FEAT_BLOCK, 0)
        part_d = lax.dynamic_slice_in_dim(down_weight, start, FEAT_BLOCK, 1)
        terms = (jnp.dot(rows_x, part_g, preferred_element_type=jnp.float32),
                 jnp.dot(rows_x, part_u, preferred_element_type=jnp.float32),
                 lax.dot_general(rows_g, part_d, trans_dims, preferred_element_type=jnp.float32))
        rounded = tuple(lax.optimization_barrier(term.astype(jnp.bfloat16)).astype(jnp.float32) for term in terms)
        return tuple(total + term for total, term in zip(carry, rounded)), None

    empty = jnp.zeros((TOKENS, FF), jnp.float32)
    (gate, upper, back), _ = lax.scan(block_step, (empty, empty, empty), jnp.arange(N_COL, dtype=jnp.int32))
    sig = jax.nn.sigmoid(gate)
    silu = gate * sig
    hidden = (silu * upper).astype(jnp.bfloat16)
    gate_delta = (back * upper * sig * (1.0 + gate * (1.0 - sig))).astype(jnp.bfloat16)
    up_delta = (back * silu).astype(jnp.bfloat16)
    first_dims = (((0,), (0,)), ((), ()))
    factor = 1.0 / (TOKENS ** 0.5)
    down_grad = (lax.dot_general(hidden, out_grad, first_dims, preferred_element_type=jnp.float32) * factor).astype(jnp.bfloat16)
    gate_grad = (lax.dot_general(acts, gate_delta, first_dims, preferred_element_type=jnp.float32) * factor).astype(jnp.bfloat16)
    up_grad = (lax.dot_general(acts, up_delta, first_dims, preferred_element_type=jnp.float32) * factor).astype(jnp.bfloat16)
    acts_grad = (lax.dot_general(gate_delta, gate_weight, trans_dims, preferred_element_type=jnp.float32)
                 + lax.dot_general(up_delta, up_weight, trans_dims, preferred_element_type=jnp.float32)).astype(jnp.bfloat16)
    return acts_grad, gate_grad, up_grad, down_grad
```

```python
import functools

import jax
import jax.numpy as jnp
from jax import lax
from jax.experimental import pallas as pl
from jax.experimental.pallas import tpu as pltpu
from jax.sharding import PartitionSpec as P

MESH = pl.DeviceIdType.MESH
BF16 = jnp.bfloat16
F32 = jnp.float32
WIDE = 256
NT = (((1,), (1,)), ((), ()))


def layer_kernel(
    chunks,
    acts_ref, logits_ref, ids_ref, head_ref, gate_ref, up_ref, down_ref,
    acts_all, grad_all, out_h, out_g, out_u, acts_grad,
    rows_in, w_gate, w_up, w_down, part, land1, land2, land3, delta,
    total, logit_buf, ids_buf, head_buf, side_send, side_land, final_buf,
    in_sem, own_sem, w_send, w_recv, x_send, x_recv, c_send, c_recv,
    s_send, s_recv, g_send, g_recv, o_local, o_send, o_recv, t_send, t_recv, xo_sem,
):
    row, col = lax.axis_index("row"), lax.axis_index("col")
    z, xh = row // 2, row % 2
    core, y, x = col % 2, (col // 2) % 4, col // 8
    g1, g2 = (y % 2 + y // 2) % 2, y // 2
    block = acts_ref.shape[0]
    half = chunks * WIDE
    mate = 1 - core
    col_x = col + 8 - 16 * x
    col_1 = x * 8 + (y + 1 - 2 * (y % 2)) * 2 + core
    col_2 = x * 8 + ((y + 3 + 2 * (y % 2)) % 4) * 2 + core
    up_z, dn_z = (z + 1) % 4, (z + 3) % 4
    peer_core = (row, col + 1 - 2 * core)
    peer_xh = (z * 2 + 1 - xh, col)
    peer_up = (up_z * 2 + xh, col)
    peer_dn = (dn_z * 2 + xh, col)

    barrier = pltpu.get_barrier_semaphore()
    for peer in (peer_core, peer_xh, peer_up, peer_dn, (row, col_x), (row, col_1), (row, col_2)):
        pl.semaphore_signal(barrier, inc=1, device_id=peer, device_id_type=MESH)

    def local(src, dst, sem):
        return pltpu.make_async_copy(src, dst, sem)

    def remote(src, dst, ssem, rsem, peer):
        return pltpu.make_async_remote_copy(
            src_ref=src, dst_ref=dst, send_sem=ssem, recv_sem=rsem, device_id=peer, device_id_type=MESH
        )

    def span(index):
        return pl.ds(pl.multiple_of(index * block, block), block)

    loads = (
        local(acts_ref, rows_in.at[0, core, span(row)], in_sem.at[0]),
        local(logits_ref, logit_buf, in_sem.at[1]),
        local(ids_ref, ids_buf, in_sem.at[2]),
        local(head_ref, head_buf, in_sem.at[3]),
    )
    for load in loads:
        load.start()

    def chunk_of(ref, side, k, by_rows):
        at = pl.ds(pl.multiple_of(side * half + k * WIDE, WIDE), WIDE)
        return ref.at[at, :] if by_rows else ref.at[:, at]

    weights = ((gate_ref, w_gate, False), (up_ref, w_up, False), (down_ref, w_down, True))

    def own_weight(k, a):
        ref, buf, by_rows = weights[a]
        return local(chunk_of(ref, core, k, by_rows), buf.at[core, k], own_sem.at[k, a])

    def sent_weight(k, a):
        ref, buf, by_rows = weights[a]
        return remote(chunk_of(ref, mate, k, by_rows), buf.at[core, k], w_send.at[k, a], w_recv.at[k, a], peer_core)

    for a in range(3):
        own_weight(0, a).start()
    pl.semaphore_wait(barrier, 7)
    for a in range(3):
        sent_weight(0, a).start()

    blocks = {
        "own": row, "mate": z * 2 + 1 - xh,
        "up": up_z * 2 + xh, "up_m": up_z * 2 + 1 - xh,
        "dn": dn_z * 2 + xh, "dn_m": dn_z * 2 + 1 - xh,
        "far": ((z + 2) % 4) * 2 + xh, "far_m": ((z + 2) % 4) * 2 + 1 - xh,
    }
    messages = (
        ("own", "mate", peer_xh),
        ("own", "dn", peer_up),
        ("own", "up", peer_dn),
        ("mate", "dn_m", peer_up),
        ("mate", "up_m", peer_dn),
        ("dn_m", "far_m", peer_up),
        ("up", "far", peer_dn),
    )

    def gather_send(t, m):
        name, _, peer = messages[m]
        ref = rows_in.at[t, core, span(blocks[name])]
        return remote(ref, ref, x_send.at[t, m], x_recv.at[t, m], peer)

    def gather_got(t, m):
        ref = rows_in.at[t, core, span(blocks[messages[m][1]])]
        remote(ref, ref, x_send.at[t, m], x_recv.at[t, m], messages[m][2]).wait_recv()

    def to_core(t, m):
        ref = rows_in.at[t, core, span(blocks["own" if m == 7 else messages[m][1]])]
        return remote(ref, ref, c_send.at[t, m], c_recv.at[t, m], peer_core)

    def from_core(t, m):
        ref = rows_in.at[t, mate, span(blocks["own" if m == 7 else messages[m][1]])]
        remote(ref, ref, c_send.at[t, m], c_recv.at[t, m], peer_core).wait_recv()

    loads[0].wait()
    for m in (0, 1, 2):
        gather_send(0, m).start()
    to_core(0, 7).start()

    for load in loads[1:]:
        load.wait()
    codes = logit_buf.shape[1]
    step_rows = 16

    def logit_step(i, carry):
        at = pl.ds(pl.multiple_of(i * step_rows, step_rows), step_rows)
        ids = ids_buf[at, :]
        code = lax.broadcasted_iota(jnp.int32, (step_rows, codes), 1)
        hit = ids[:, 0:1] == code
        for label in range(1, ids.shape[1]):
            hit = jnp.logical_or(hit, ids[:, label : label + 1] == code)
        target = jnp.where(hit, 1.0, 0.0)
        side_logit = (jax.nn.sigmoid(logit_buf[at, :]) - target).astype(BF16)
        rows_in[1, core, pl.ds(pl.multiple_of(row * block + i * step_rows, step_rows), step_rows), :] = jnp.dot(
            side_logit, head_buf[...], preferred_element_type=F32
        ).astype(BF16)
        return carry

    lax.fori_loop(0, block // step_rows, logit_step, 0)
    for m in (0, 1, 2):
        gather_send(1, m).start()
    to_core(1, 7).start()

    def gather_rest(t):
        gather_got(t, 0)
        for m in (3, 4):
            gather_send(t, m).start()
        gather_got(t, 2)
        gather_send(t, 6).start()
        gather_got(t, 3)
        gather_send(t, 5).start()
        for m in (0, 2, 3):
            to_core(t, m).start()
        for m in (1, 4, 5, 6):
            gather_got(t, m)
            to_core(t, m).start()

    total[...] = jnp.zeros_like(total)
    gather_rest(0)

    def more_weights(k, carry):
        for a in range(3):
            own_weight(k, a).start()
            sent_weight(k, a).start()
        return carry

    lax.fori_loop(1, chunks, more_weights, 0)
    for m in range(8):
        from_core(0, m)

    def peer_of(dim):
        return (row, jnp.where(dim == 0, col_x, jnp.where(dim == 1, col_1, col_2)))

    def turn(k, a):
        return (k + a) % 3

    def slot_of(k, a, b):
        r = turn(k, a)
        bits = ((b // 4 + x) % 2, ((b // 2) % 2 + g1) % 2, (b % 2 + g2) % 2)
        slot = 0
        for dim, bit in enumerate(bits):
            e = (dim - r + 3) % 3
            slot = slot + bit * (4 - 2 * e + e * (e - 1) // 2)
        return slot

    def sum_send(step, k, a):
        size = (4, 2, 1)[step] * block
        dst = (land1, land2, land3)[step]
        return remote(
            part.at[k, a, pl.ds(size, size)], dst.at[k, a], s_send.at[step, k, a], s_recv.at[step, k, a],
            peer_of((turn(k, a) + step) % 3),
        )

    def give_send(step, k, a):
        size = (4, 2, 1)[step] * block
        return remote(
            delta.at[k, a, pl.ds(0, size)], delta.at[k, a, pl.ds(size, size)], g_send.at[step, k, a], g_recv.at[step, k, a],
            peer_of((turn(k, a) + step) % 3),
        )

    def got_weight(k, a):
        own_weight(k, a).wait()
        sent_weight(k, a).wait_recv()

    def place(k, a, value):
        for b in range(8):
            part[k, a, span(slot_of(k, a, b)), :] = value[b * block : (b + 1) * block].astype(BF16)
        sum_send(0, k, a).start()

    def forward_in(k):
        for a, buf in ((0, w_gate), (1, w_up)):
            got_weight(k, a)
            value = jnp.dot(rows_in[0, 0], buf[0, k], preferred_element_type=F32)
            value = value + jnp.dot(rows_in[0, 1], buf[1, k], preferred_element_type=F32)
            place(k, a, value)

    def forward_out(k):
        got_weight(k, 2)
        value = lax.dot_general(rows_in[1, 0], w_down[0, k], NT, preferred_element_type=F32)
        value = value + lax.dot_general(rows_in[1, 1], w_down[1, k], NT, preferred_element_type=F32)
        place(k, 2, value)

    forward_in(0)
    gather_rest(1)
    for m in range(8):
        from_core(1, m)
    outs_x = (
        local(rows_in.at[0, core], acts_all, xo_sem.at[0]),
        local(rows_in.at[1, core], grad_all, xo_sem.at[1]),
    )
    for copy in outs_x:
        copy.start()

    def add_in(k, a, land, first, count):
        for b in range(first, first + count):
            at = pl.ds(b * block, block)
            part[k, a, at, :] = part[k, a, at, :] + land[k, a, at, :]

    def sum_stage(step, k):
        land = (land1, land2)[step]
        keep = (2, 1)[step]
        for a in range(3):
            sum_send(step, k, a).wait_recv()
            add_in(k, a, land, keep, keep)
            sum_send(step + 1, k, a).start()
            add_in(k, a, land, 0, keep)

    def activate(k):
        for a in range(3):
            sum_send(2, k, a).wait_recv()
        piece = 32

        def act_step(i, carry):
            at = pl.ds(pl.multiple_of(i * piece, piece), piece)
            gate, upper, back = (part[k, a, at, :].astype(F32) + land3[k, a, at, :].astype(F32) for a in range(3))
            sig = jax.nn.sigmoid(gate)
            silu = gate * sig
            delta[k, 0, at, :] = (back * upper * sig * (1.0 + gate * (1.0 - sig))).astype(BF16)
            delta[k, 1, at, :] = (back * silu).astype(BF16)
            delta[k, 2, at, :] = (silu * upper).astype(BF16)
            return carry

        lax.fori_loop(0, block // piece, act_step, 0)
        for a in range(3):
            give_send(2, k, a).start()

    def give_stage(step, k, arrays):
        for a in range(3):
            give_send(step, k, a).wait_recv()
            if a in arrays:
                give_send(step - 1, k, a).start()

    outs = (out_g, out_u, out_h)

    def own_out(k, a):
        return local(part.at[k, a], chunk_of(outs[a], core, k, False), o_local.at[k, a])

    def core_out(k, a):
        return remote(part.at[k, a], chunk_of(outs[a], core, k, False), o_send.at[k, a], o_recv.at[k, a], peer_core)

    def core_out_got(k, a):
        ref = chunk_of(outs[a], mate, k, False)
        remote(part.at[k, a], ref, o_send.at[k, a], o_recv.at[k, a], peer_core).wait_recv()

    def finish(k, a):
        give_send(0, k, a).wait_recv()
        for step in range(3):
            sum_send(step, k, a).wait_send()
        for b in range(8):
            part[k, a, pl.ds(b * block, block), :] = delta[k, a, span(slot_of(k, a, b)), :]
        own_out(k, a).start()
        core_out(k, a).start()

    def backward(k):
        for a in range(2):
            finish(k, a)
        for h in range(2):
            total[h] = (
                total[h]
                + lax.dot_general(part[k, 0], w_gate[h, k], NT, preferred_element_type=F32)
                + lax.dot_general(part[k, 1], w_up[h, k], NT, preferred_element_type=F32)
            )

    def slot_step(i, carry):
        @pl.when(i < chunks)
        def _():
            forward_out(i)

        @pl.when(i + 1 < chunks)
        def _():
            forward_in(i + 1)

        def stage(lag, run):
            @pl.when(jnp.logical_and(i >= lag, i < chunks + lag))
            def _():
                run(i - lag)

        stage(1, functools.partial(sum_stage, 0))
        stage(2, functools.partial(sum_stage, 1))
        stage(3, activate)
        stage(4, lambda k: give_stage(2, k, (0, 1, 2)))
        stage(5, lambda k: give_stage(1, k, (0, 1)))
        stage(6, backward)

        @pl.when(i >= chunks + 4)
        def _():
            give_send(0, i - chunks - 4, 2).start()

        return carry

    lax.fori_loop(0, chunks + 6, slot_step, 0)

    def late_send(k, carry):
        give_send(0, k, 2).start()
        return carry

    lax.fori_loop(2, chunks, late_send, 0)

    def side(m, src, peer):
        return remote(src, side_land.at[m], t_send.at[m], t_recv.at[m], peer)

    def to_mate(b, carry):
        at = span(b)
        side_send[at, :] = total[mate, at, :].astype(BF16)
        return carry

    lax.fori_loop(0, 8, to_mate, 0)
    core_copy = remote(side_send, final_buf, t_send.at[7], t_recv.at[7], peer_core)
    core_copy.start()
    core_copy.wait()

    def add_mate(b, carry):
        at = span(b)
        total[core, at, :] = total[core, at, :] + final_buf[at, :].astype(F32)
        side_send[at, :] = total[core, at, :].astype(BF16)
        return carry

    lax.fori_loop(0, 8, add_mate, 0)

    def held(name):
        return span(blocks[name])

    def send_block(m, name, peer):
        return side(m, side_send.at[held(name)], peer)

    far_up = send_block(0, "far", peer_up)
    far_dn = send_block(1, "far_m", peer_dn)
    one_up = send_block(2, "up_m", peer_up)
    one_dn = send_block(3, "dn", peer_dn)
    for copy in (far_up, far_dn, one_up, one_dn):
        copy.start()
    far_up.wait_recv()
    side_send[held("up"), :] = (total[core, held("up"), :] + side_land[0].astype(F32)).astype(BF16)
    two_up = send_block(4, "up", peer_up)
    two_up.start()
    far_dn.wait_recv()
    side_send[held("dn_m"), :] = (total[core, held("dn_m"), :] + side_land[1].astype(F32)).astype(BF16)
    two_dn = send_block(5, "dn_m", peer_dn)
    two_dn.start()
    one_up.wait_recv()
    two_dn.wait_recv()
    side_send[held("mate"), :] = (
        total[core, held("mate"), :] + side_land[2].astype(F32) + side_land[5].astype(F32)
    ).astype(BF16)
    swap = send_block(6, "mate", peer_xh)
    swap.start()
    one_dn.wait_recv()
    two_up.wait_recv()
    kept = total[core, held("own"), :] + side_land[3].astype(F32) + side_land[4].astype(F32)
    swap.wait_recv()
    side_send[held("own"), :] = (kept + side_land[6].astype(F32)).astype(BF16)
    result = local(side_send.at[held("own")], acts_grad, xo_sem.at[2])
    result.start()

    def last(k, carry):
        finish(k, 2)
        return carry

    lax.fori_loop(0, chunks, last, 0)

    def drain(k, carry):
        for a in range(3):
            sent_weight(k, a).wait_send()
            own_out(k, a).wait()
            core_out(k, a).wait_send()
            core_out_got(k, a)
            for step in range(3):
                give_send(step, k, a).wait_send()
        return carry

    lax.fori_loop(0, chunks, drain, 0)
    for t in range(2):
        for m in range(7):
            gather_send(t, m).wait_send()
        for m in range(8):
            to_core(t, m).wait_send()
        outs_x[t].wait()
    for copy in (far_up, far_dn, one_up, one_dn, two_up, two_dn, swap):
        copy.wait_send()
    result.wait()


def per_device(acts, logits, label_ids, head_weight, gate_weight, up_weight, down_weight):
    tokens = acts.shape[0] * 8
    width, feats = gate_weight.shape[1], acts.shape[1]
    block = acts.shape[0]
    chunks = width // 2 // WIDE
    any_spec = pl.BlockSpec(memory_space=pl.ANY)
    dma = pltpu.SemaphoreType.DMA
    hidden_shape = jax.ShapeDtypeStruct((tokens, width), BF16)
    rows_shape = jax.ShapeDtypeStruct((tokens, feats), BF16)
    acts_all, grad_all, hidden, gate_delta, up_delta, acts_grad = pl.pallas_call(
        functools.partial(layer_kernel, chunks),
        out_shape=(rows_shape, rows_shape, hidden_shape, hidden_shape, hidden_shape, jax.ShapeDtypeStruct(acts.shape, BF16)),
        in_specs=[any_spec] * 7,
        out_specs=(any_spec,) * 6,
        scratch_shapes=[
            pltpu.VMEM((2, 2, tokens, feats), BF16),
            pltpu.VMEM((2, chunks, feats, WIDE), BF16),
            pltpu.VMEM((2, chunks, feats, WIDE), BF16),
            pltpu.VMEM((2, chunks, WIDE, feats), BF16),
            pltpu.VMEM((chunks, 3, tokens, WIDE), BF16),
            pltpu.VMEM((chunks, 3, 4 * block, WIDE), BF16),
            pltpu.VMEM((chunks, 3, 2 * block, WIDE), BF16),
            pltpu.VMEM((chunks, 3, block, WIDE), BF16),
            pltpu.VMEM((chunks, 3, tokens, WIDE), BF16),
            pltpu.VMEM((2, tokens, feats), F32),
            pltpu.VMEM(logits.shape, F32),
            pltpu.VMEM(label_ids.shape, jnp.int32),
            pltpu.VMEM(head_weight.shape, BF16),
            pltpu.VMEM((tokens, feats), BF16),
            pltpu.VMEM((7, block, feats), BF16),
            pltpu.VMEM((tokens, feats), BF16),
            dma((4,)), dma((chunks, 3)), dma((chunks, 3)), dma((chunks, 3)),
            dma((2, 7)), dma((2, 7)), dma((2, 8)), dma((2, 8)),
            dma((3, chunks, 3)), dma((3, chunks, 3)), dma((3, chunks, 3)), dma((3, chunks, 3)),
            dma((chunks, 3)), dma((chunks, 3)), dma((chunks, 3)), dma((8,)), dma((8,)), dma((3,)),
        ],
        compiler_params=pltpu.CompilerParams(collective_id=0, has_side_effects=True, vmem_limit_bytes=60 * 2**20),
        name="layer_kernel",
    )(acts, logits, label_ids, head_weight, gate_weight, up_weight, down_weight)
    first_dims = (((0,), (0,)), ((), ()))
    factor = 1.0 / tokens**0.5

    def weight_grad(left, right):
        return (lax.dot_general(left, right, first_dims, preferred_element_type=F32) * factor).astype(BF16)

    return acts_grad, weight_grad(acts_all, gate_delta), weight_grad(acts_all, up_delta), weight_grad(hidden, grad_all)


def solution(mesh):
    placed = (
        P("row", "col"),
        P("row", None),
        P("row", None),
        P(None, "col"),
        P("col", "row"),
        P("col", "row"),
        P("row", "col"),
    )
    return jax.shard_map(
        per_device,
        mesh=mesh,
        in_specs=placed,
        out_specs=(P("row", "col"), P("col", "row"), P("col", "row"), P("row", "col")),
        check_vma=False,
    )
```

```python
import functools

import jax
import jax.numpy as jnp
from jax import lax
from jax.experimental import pallas as pl
from jax.experimental.pallas import tpu as pltpu
from jax.sharding import PartitionSpec as P

MESH = pl.DeviceIdType.MESH
BF16 = jnp.bfloat16
F32 = jnp.float32
WIDE = 256
NT = (((1,), (1,)), ((), ()))


def layer_kernel(
    chunks,
    acts_ref, logits_ref, ids_ref, head_ref, gate_ref, up_ref, down_ref,
    acts_turned, grad_all, out_h, out_g, out_u, acts_grad,
    rows_in, w_gate, w_up, w_down, part, land1, land2, land3, delta,
    total, logit_buf, ids_buf, head_buf, logit_grad, turned, hidden_turned,
    mate_send, mate_land, side_send, side_land,
    in_sem, own_sem, w_send, w_recv, x_send, x_recv, c_send, c_recv,
    s_send, s_recv, g_send, g_recv, o_local, o_send, o_recv, t_send, t_recv, xo_sem,
):
    row, col = lax.axis_index("row"), lax.axis_index("col")
    z, xh = row // 2, row % 2
    core, y, x = col % 2, (col // 2) % 4, col // 8
    g1, g2 = (y % 2 + y // 2) % 2, y // 2
    block = acts_ref.shape[0]
    half = chunks * WIDE
    feats = acts_ref.shape[1]
    mate = 1 - core
    col_x = col + 8 - 16 * x
    col_1 = x * 8 + (y + 1 - 2 * (y % 2)) * 2 + core
    col_2 = x * 8 + ((y + 3 + 2 * (y % 2)) % 4) * 2 + core
    up_z, dn_z = (z + 1) % 4, (z + 3) % 4
    peer_core = (row, col + 1 - 2 * core)
    peer_xh = (z * 2 + 1 - xh, col)
    peer_up = (up_z * 2 + xh, col)
    peer_dn = (dn_z * 2 + xh, col)

    barrier = pltpu.get_barrier_semaphore()
    for peer in (peer_core, peer_xh, peer_up, peer_dn, (row, col_x), (row, col_1), (row, col_2)):
        pl.semaphore_signal(barrier, inc=1, device_id=peer, device_id_type=MESH)

    def local(src, dst, sem):
        return pltpu.make_async_copy(src, dst, sem)

    def remote(src, dst, ssem, rsem, peer):
        return pltpu.make_async_remote_copy(
            src_ref=src, dst_ref=dst, send_sem=ssem, recv_sem=rsem, device_id=peer, device_id_type=MESH
        )

    def span(index):
        return pl.ds(pl.multiple_of(index * block, block), block)

    def side_of(index):
        return pl.ds(pl.multiple_of(index * feats, feats), feats)

    loads = (
        local(acts_ref, rows_in.at[0, span(row), side_of(core)], in_sem.at[0]),
        local(logits_ref, logit_buf, in_sem.at[1]),
        local(ids_ref, ids_buf, in_sem.at[2]),
        local(head_ref, head_buf, in_sem.at[3]),
    )
    for load in loads:
        load.start()

    def chunk_of(ref, side, k, by_rows):
        at = pl.ds(pl.multiple_of(side * half + k * WIDE, WIDE), WIDE)
        return ref.at[at, :] if by_rows else ref.at[:, at]

    def weight_side(buf, k, by_rows):
        return buf.at[k, :, side_of(core)] if by_rows else buf.at[k, side_of(core), :]

    weights = ((gate_ref, w_gate, False), (up_ref, w_up, False), (down_ref, w_down, True))

    def own_weight(k, a):
        ref, buf, by_rows = weights[a]
        return local(chunk_of(ref, core, k, by_rows), weight_side(buf, k, by_rows), own_sem.at[k, a])

    def sent_weight(k, a):
        ref, buf, by_rows = weights[a]
        return remote(
            chunk_of(ref, mate, k, by_rows), weight_side(buf, k, by_rows), w_send.at[k, a], w_recv.at[k, a], peer_core
        )

    def start_own(k, carry):
        for a in range(3):
            own_weight(k, a).start()
        return carry

    def start_sent(k, carry):
        for a in range(3):
            sent_weight(k, a).start()
        return carry

    lax.fori_loop(0, chunks, start_own, 0)
    pl.semaphore_wait(barrier, 7)

    blocks = {
        "own": row, "mate": z * 2 + 1 - xh,
        "up": up_z * 2 + xh, "up_m": up_z * 2 + 1 - xh,
        "dn": dn_z * 2 + xh, "dn_m": dn_z * 2 + 1 - xh,
        "far": ((z + 2) % 4) * 2 + xh, "far_m": ((z + 2) % 4) * 2 + 1 - xh,
    }
    messages = (
        ("own", "mate", peer_xh),
        ("own", "dn", peer_up),
        ("own", "up", peer_dn),
        ("mate", "dn_m", peer_up),
        ("mate", "up_m", peer_dn),
        ("dn_m", "far_m", peer_up),
        ("up", "far", peer_dn),
    )

    def gather_send(t, m):
        name, _, peer = messages[m]
        ref = rows_in.at[t, span(blocks[name]), side_of(core)]
        return remote(ref, ref, x_send.at[t, m], x_recv.at[t, m], peer)

    def gather_got(t, m):
        ref = rows_in.at[t, span(blocks[messages[m][1]]), side_of(core)]
        remote(ref, ref, x_send.at[t, m], x_recv.at[t, m], messages[m][2]).wait_recv()

    def to_core(t, m):
        ref = rows_in.at[t, span(blocks["own" if m == 7 else messages[m][1]]), side_of(core)]
        return remote(ref, ref, c_send.at[t, m], c_recv.at[t, m], peer_core)

    def from_core(t, m):
        ref = rows_in.at[t, span(blocks["own" if m == 7 else messages[m][1]]), side_of(mate)]
        remote(ref, ref, c_send.at[t, m], c_recv.at[t, m], peer_core).wait_recv()

    loads[0].wait()
    for m in (0, 1, 2):
        gather_send(0, m).start()
    to_core(0, 7).start()
    lax.fori_loop(0, chunks, start_sent, 0)

    for load in loads[1:]:
        load.wait()
    codes = logit_buf.shape[1]
    step_rows = 16

    def logit_step(i, carry):
        at = pl.ds(pl.multiple_of(i * step_rows, step_rows), step_rows)
        ids = ids_buf[at, :]
        code = lax.broadcasted_iota(jnp.int32, (step_rows, codes), 1)
        hit = ids[:, 0:1] == code
        for label in range(1, ids.shape[1]):
            hit = jnp.logical_or(hit, ids[:, label : label + 1] == code)
        target = jnp.where(hit, 1.0, 0.0)
        logit_grad[at, :] = (jax.nn.sigmoid(logit_buf[at, :]) - target).astype(BF16)
        return carry

    lax.fori_loop(0, block // step_rows, logit_step, 0)
    rows_in[1, span(row), side_of(core)] = jnp.dot(
        logit_grad[...], head_buf[...], preferred_element_type=F32
    ).astype(BF16)
    for m in (0, 1, 2):
        gather_send(1, m).start()
    to_core(1, 7).start()

    def gather_rest(t):
        gather_got(t, 2)
        gather_send(t, 6).start()
        gather_got(t, 0)
        for m in (3, 4):
            gather_send(t, m).start()
        for m in (2, 0):
            to_core(t, m).start()
        gather_got(t, 1)
        to_core(t, 1).start()
        gather_got(t, 3)
        gather_send(t, 5).start()
        to_core(t, 3).start()
        for m in (6, 4, 5):
            gather_got(t, m)
            to_core(t, m).start()

    total[...] = jnp.zeros_like(total)
    gather_rest(0)
    for m in range(8):
        from_core(0, m)

    def peer_of(dim):
        return (row, jnp.where(dim == 0, col_x, jnp.where(dim == 1, col_1, col_2)))

    def turn(k, a):
        return (k + a) % 3

    def slot_of(k, a, b):
        r = turn(k, a)
        bits = ((b // 4 + x) % 2, ((b // 2) % 2 + g1) % 2, (b % 2 + g2) % 2)
        slot = 0
        for dim, bit in enumerate(bits):
            e = (dim - r + 3) % 3
            slot = slot + bit * (4 - 2 * e + e * (e - 1) // 2)
        return slot

    def sum_send(step, k, a):
        size = (4, 2, 1)[step] * block
        dst = (land1, land2, land3)[step]
        return remote(
            part.at[k, a, pl.ds(size, size)], dst.at[k, a], s_send.at[step, k, a], s_recv.at[step, k, a],
            peer_of((turn(k, a) + step) % 3),
        )

    def give_send(step, k, a):
        size = (4, 2, 1)[step] * block
        return remote(
            delta.at[k, a, pl.ds(0, size)], delta.at[k, a, pl.ds(size, size)], g_send.at[step, k, a], g_recv.at[step, k, a],
            peer_of((turn(k, a) + step) % 3),
        )

    def got_weight(k, a):
        own_weight(k, a).wait()
        sent_weight(k, a).wait_recv()

    def place(k, a, value):
        for b in range(8):
            part[k, a, span(slot_of(k, a, b)), :] = value[b * block : (b + 1) * block].astype(BF16)
        sum_send(0, k, a).start()

    def forward_in(k):
        for a, buf in ((0, w_gate), (1, w_up)):
            got_weight(k, a)
            place(k, a, jnp.dot(rows_in[0], buf[k], preferred_element_type=F32))

    def forward_out(k):
        got_weight(k, 2)
        place(k, 2, lax.dot_general(rows_in[1], w_down[k], NT, preferred_element_type=F32))

    ahead = min(3, chunks)

    def first_chunks(k, carry):
        forward_in(k)
        return carry

    lax.fori_loop(0, ahead, first_chunks, 0)
    gather_rest(1)
    for m in range(8):
        from_core(1, m)

    def add_in(k, a, land, first, count):
        for b in range(first, first + count):
            at = pl.ds(b * block, block)
            part[k, a, at, :] = part[k, a, at, :] + land[k, a, at, :]

    def sum_stage(step, k):
        land = (land1, land2)[step]
        keep = (2, 1)[step]
        for a in range(3):
            sum_send(step, k, a).wait_recv()
            add_in(k, a, land, keep, keep)
            sum_send(step + 1, k, a).start()
            add_in(k, a, land, 0, keep)

    def activate(k):
        for a in range(3):
            sum_send(2, k, a).wait_recv()
        piece = 32

        def act_step(i, carry):
            at = pl.ds(pl.multiple_of(i * piece, piece), piece)
            gate, upper, back = (part[k, a, at, :].astype(F32) + land3[k, a, at, :].astype(F32) for a in range(3))
            sig = jax.nn.sigmoid(gate)
            silu = gate * sig
            delta[k, 0, at, :] = (back * upper * sig * (1.0 + gate * (1.0 - sig))).astype(BF16)
            delta[k, 1, at, :] = (back * silu).astype(BF16)
            delta[k, 2, at, :] = (silu * upper).astype(BF16)
            return carry

        lax.fori_loop(0, block // piece, act_step, 0)
        for a in range(3):
            give_send(2, k, a).start()

    def give_stage(step, k, arrays=(0, 1)):
        for a in arrays:
            give_send(step, k, a).wait_recv()
            give_send(step - 1, k, a).start()

    outs = (out_g, out_u, out_h)

    def own_out(k, a):
        src = hidden_turned.at[k] if a == 2 else part.at[k, a]
        return local(src, chunk_of(outs[a], core, k, a == 2), o_local.at[k, a])

    def core_out(k, a, side=core):
        src = hidden_turned.at[k] if a == 2 else part.at[k, a]
        return remote(src, chunk_of(outs[a], side, k, a == 2), o_send.at[k, a], o_recv.at[k, a], peer_core)

    def finish(k, a):
        give_send(0, k, a).wait_recv()
        for step in range(3):
            sum_send(step, k, a).wait_send()
        for b in range(8):
            part[k, a, pl.ds(b * block, block), :] = delta[k, a, span(slot_of(k, a, b)), :]
        if a == 2:
            tokens = 8 * block
            for at in range(0, tokens, 128):
                hidden_turned[k, :, at : at + 128] = part[k, 2, at : at + 128, :].T
        own_out(k, a).start()
        core_out(k, a).start()

    def backward(k):
        for a in range(2):
            finish(k, a)
        total[...] = (
            total[...]
            + lax.dot_general(part[k, 0], w_gate[k], NT, preferred_element_type=F32)
            + lax.dot_general(part[k, 1], w_up[k], NT, preferred_element_type=F32)
        )

    grad_copy = local(rows_in.at[1, :, side_of(core)], grad_all, xo_sem.at[0])
    turned_copy = local(turned, acts_turned, xo_sem.at[1])

    def turn_inputs():
        grad_copy.start()
        for at in range(0, feats, 128):
            column = pl.ds(pl.multiple_of(core * feats + at, 128), 128)
            turned[at : at + 128, :] = rows_in[0, :, column].T
        turned_copy.start()

    def late_give(first, last):
        def step(k, carry):
            give_stage(1, k, (2,))
            return carry

        lax.fori_loop(min(first, chunks), min(last, chunks), step, 0)

    def slot_step(i, carry):
        @pl.when(i < chunks)
        def _():
            forward_out(i)

        @pl.when(i + ahead < chunks)
        def _():
            forward_in(i + ahead)

        def stage(lag, run):
            @pl.when(jnp.logical_and(i >= lag, i < chunks + lag))
            def _():
                run(i - lag)

        stage(1, functools.partial(sum_stage, 0))
        stage(2, functools.partial(sum_stage, 1))
        stage(3, activate)
        stage(4, functools.partial(give_stage, 2))
        stage(5, functools.partial(give_stage, 1))
        stage(6, backward)

        @pl.when(i == 0)
        def _():
            turn_inputs()

        @pl.when(i >= chunks + 1)
        def _():
            first = 2 * (i - chunks - 1)
            for k in (first, first + 1):
                @pl.when(k < chunks)
                def _():
                    give_stage(2, k, (2,))

        @pl.when(i == chunks + 4)
        def _():
            late_give(0, 3)

        return carry

    lax.fori_loop(0, chunks + 6, slot_step, 0)

    def late_finish(first, last):
        def step(k, carry):
            finish(k, 2)
            return carry

        lax.fori_loop(min(first, chunks), min(last, chunks), step, 0)

    def pair_copy(number, at_z):
        at = pl.ds(pl.multiple_of(at_z * 2 * block, 2 * block), 2 * block)
        return at, remote(mate_send.at[at], mate_land.at[at], t_send.at[7 + number], t_recv.at[7 + number], peer_core)

    pairs = [pair_copy(number, at_z) for number, at_z in enumerate(((z + 2) % 4, up_z, dn_z, z))]
    for at, copy in pairs:
        mate_send[at, :] = total[at, side_of(mate)].astype(BF16)
        copy.start()

    def pair_sum(number):
        at, copy = pairs[number]
        copy.wait_recv()
        total[at, side_of(core)] = total[at, side_of(core)] + mate_land[at, :].astype(F32)
        if number < 3:
            side_send[at, :] = total[at, side_of(core)].astype(BF16)

    def held(name):
        return span(blocks[name])

    def mine(name):
        return total[held(name), side_of(core)]

    def send_block(m, name, peer):
        return remote(side_send.at[held(name)], side_land.at[m], t_send.at[m], t_recv.at[m], peer)

    far_up = send_block(0, "far", peer_up)
    far_dn = send_block(1, "far_m", peer_dn)
    one_up = send_block(2, "up_m", peer_up)
    one_dn = send_block(3, "dn", peer_dn)
    two_up = send_block(4, "up", peer_up)
    two_dn = send_block(5, "dn_m", peer_dn)
    swap = send_block(6, "mate", peer_xh)
    pair_sum(0)
    far_up.start()
    far_dn.start()
    pair_sum(1)
    one_up.start()
    pair_sum(2)
    one_dn.start()
    pair_sum(3)
    late_give(3, 5)
    far_up.wait_recv()
    side_send[held("up"), :] = (mine("up") + side_land[0].astype(F32)).astype(BF16)
    two_up.start()
    far_dn.wait_recv()
    side_send[held("dn_m"), :] = (mine("dn_m") + side_land[1].astype(F32)).astype(BF16)
    two_dn.start()
    late_give(5, chunks)
    late_finish(0, 1)
    one_up.wait_recv()
    two_dn.wait_recv()
    side_send[held("mate"), :] = (mine("mate") + side_land[2].astype(F32) + side_land[5].astype(F32)).astype(BF16)
    swap.start()
    late_finish(1, chunks - 1)
    one_dn.wait_recv()
    two_up.wait_recv()
    kept = mine("own") + side_land[3].astype(F32) + side_land[4].astype(F32)
    swap.wait_recv()
    side_send[held("own"), :] = (kept + side_land[6].astype(F32)).astype(BF16)
    result = local(side_send.at[held("own")], acts_grad, xo_sem.at[2])
    result.start()
    late_finish(chunks - 1, chunks)

    def drain(k, carry):
        for a in range(3):
            sent_weight(k, a).wait_send()
            own_out(k, a).wait()
            core_out(k, a).wait_send()
            core_out(k, a, mate).wait_recv()
            for step in range(3):
                give_send(step, k, a).wait_send()
        return carry

    lax.fori_loop(0, chunks, drain, 0)
    for t in range(2):
        for m in range(7):
            gather_send(t, m).wait_send()
        for m in range(8):
            to_core(t, m).wait_send()
    grad_copy.wait()
    turned_copy.wait()
    for _, copy in pairs:
        copy.wait_send()
    for copy in (far_up, far_dn, one_up, one_dn, two_up, two_dn, swap):
        copy.wait_send()
    result.wait()


def per_device(acts, logits, label_ids, head_weight, gate_weight, up_weight, down_weight):
    tokens = acts.shape[0] * 8
    width, feats = gate_weight.shape[1], acts.shape[1]
    block = acts.shape[0]
    chunks = width // 2 // WIDE
    any_spec = pl.BlockSpec(memory_space=pl.ANY)
    dma = pltpu.SemaphoreType.DMA
    hidden_shape = jax.ShapeDtypeStruct((tokens, width), BF16)
    rows_shape = jax.ShapeDtypeStruct((tokens, feats), BF16)
    turned, grad_all, hidden, gate_delta, up_delta, acts_grad = pl.pallas_call(
        functools.partial(layer_kernel, chunks),
        out_shape=(
            jax.ShapeDtypeStruct((feats, tokens), BF16), rows_shape, jax.ShapeDtypeStruct((width, tokens), BF16),
            hidden_shape, hidden_shape, jax.ShapeDtypeStruct(acts.shape, BF16),
        ),
        in_specs=[any_spec] * 7,
        out_specs=(any_spec,) * 6,
        scratch_shapes=[
            pltpu.VMEM((2, tokens, 2 * feats), BF16),
            pltpu.VMEM((chunks, 2 * feats, WIDE), BF16),
            pltpu.VMEM((chunks, 2 * feats, WIDE), BF16),
            pltpu.VMEM((chunks, WIDE, 2 * feats), BF16),
            pltpu.VMEM((chunks, 3, tokens, WIDE), BF16),
            pltpu.VMEM((chunks, 3, 4 * block, WIDE), BF16),
            pltpu.VMEM((chunks, 3, 2 * block, WIDE), BF16),
            pltpu.VMEM((chunks, 3, block, WIDE), BF16),
            pltpu.VMEM((chunks, 3, tokens, WIDE), BF16),
            pltpu.VMEM((tokens, 2 * feats), F32),
            pltpu.VMEM(logits.shape, F32),
            pltpu.VMEM(label_ids.shape, jnp.int32),
            pltpu.VMEM(head_weight.shape, BF16),
            pltpu.VMEM(logits.shape, BF16),
            pltpu.VMEM((feats, tokens), BF16),
            pltpu.VMEM((chunks, WIDE, tokens), BF16),
            pltpu.VMEM((tokens, feats), BF16),
            pltpu.VMEM((tokens, feats), BF16),
            pltpu.VMEM((tokens, feats), BF16),
            pltpu.VMEM((7, block, feats), BF16),
            dma((4,)), dma((chunks, 3)), dma((chunks, 3)), dma((chunks, 3)),
            dma((2, 7)), dma((2, 7)), dma((2, 8)), dma((2, 8)),
            dma((3, chunks, 3)), dma((3, chunks, 3)), dma((3, chunks, 3)), dma((3, chunks, 3)),
            dma((chunks, 3)), dma((chunks, 3)), dma((chunks, 3)), dma((11,)), dma((11,)), dma((3,)),
        ],
        compiler_params=pltpu.CompilerParams(collective_id=0, has_side_effects=True, vmem_limit_bytes=60 * 2**20),
        name="layer_kernel",
    )(acts, logits, label_ids, head_weight, gate_weight, up_weight, down_weight)
    factor = 1.0 / tokens**0.5

    def weight_grad(left, right):
        return (jnp.dot(left, right, preferred_element_type=F32) * factor).astype(BF16)

    return acts_grad, weight_grad(turned, gate_delta), weight_grad(turned, up_delta), weight_grad(hidden, grad_all)


def solution(mesh):
    placed = (
        P("row", "col"),
        P("row", None),
        P("row", None),
        P(None, "col"),
        P("col", "row"),
        P("col", "row"),
        P("row", "col"),
    )
    return jax.shard_map(
        per_device,
        mesh=mesh,
        in_specs=placed,
        out_specs=(P("row", "col"), P("col", "row"), P("col", "row"), P("row", "col")),
        check_vma=False,
    )
```

```python
import functools

import jax
import jax.numpy as jnp
from jax import lax
from jax.experimental import pallas as pl
from jax.experimental.pallas import tpu as pltpu
from jax.sharding import PartitionSpec as P

MESH = pl.DeviceIdType.MESH
BF16 = jnp.bfloat16
F32 = jnp.float32
WIDE = 256
NT = (((1,), (1,)), ((), ()))
ORDER = ("own", "up", "dn", "mate", "far", "up_m", "dn_m", "far_m")
MESSAGES = (
    ("own", "mate", "xh"),
    ("own", "dn", "up"),
    ("own", "up", "dn"),
    ("mate", "dn_m", "up"),
    ("mate", "up_m", "dn"),
    ("dn_m", "far_m", "up"),
    ("up", "far", "dn"),
)


def layer_kernel(
    chunks,
    acts_ref, logits_ref, ids_ref, head_ref, gate_ref, up_ref, down_ref,
    acts_turned, grad_all, out_h, out_g, out_u, acts_grad,
    rows_in, w_gate, w_up, w_down, part, land1, land2, land3, delta,
    total, logit_buf, ids_buf, head_buf, logit_grad, turned, hidden_turned,
    mate_send, mate_land, side_send, side_land,
    in_sem, own_sem, w_send, w_recv, x_send, x_recv, c_send, c_recv,
    s_send, s_recv, g_send, g_recv, o_local, o_send, o_recv, t_send, t_recv, xo_sem,
):
    row, col = lax.axis_index("row"), lax.axis_index("col")
    z, xh = row // 2, row % 2
    core, y, x = col % 2, (col // 2) % 4, col // 8
    g1, g2 = (y % 2 + y // 2) % 2, y // 2
    block = acts_ref.shape[0]
    half = chunks * WIDE
    feats = acts_ref.shape[1]
    mate = 1 - core
    col_x = col + 8 - 16 * x
    col_1 = x * 8 + (y + 1 - 2 * (y % 2)) * 2 + core
    col_2 = x * 8 + ((y + 3 + 2 * (y % 2)) % 4) * 2 + core
    up_z, dn_z = (z + 1) % 4, (z + 3) % 4
    peer_core = (row, col + 1 - 2 * core)
    peer_xh = (z * 2 + 1 - xh, col)
    peer_up = (up_z * 2 + xh, col)
    peer_dn = (dn_z * 2 + xh, col)

    barrier = pltpu.get_barrier_semaphore()
    for peer in (peer_core, peer_xh, peer_up, peer_dn, (row, col_x), (row, col_1), (row, col_2)):
        pl.semaphore_signal(barrier, inc=1, device_id=peer, device_id_type=MESH)

    def local(src, dst, sem):
        return pltpu.make_async_copy(src, dst, sem)

    def remote(src, dst, ssem, rsem, peer):
        return pltpu.make_async_remote_copy(
            src_ref=src, dst_ref=dst, send_sem=ssem, recv_sem=rsem, device_id=peer, device_id_type=MESH
        )

    def span(index):
        return pl.ds(pl.multiple_of(index * block, block), block)

    def held(name):
        return pl.ds(ORDER.index(name) * block, block)

    def side_of(index):
        return pl.ds(pl.multiple_of(index * feats, feats), feats)

    loads = (
        local(acts_ref, rows_in.at[0, held("own"), side_of(core)], in_sem.at[0]),
        local(logits_ref, logit_buf, in_sem.at[1]),
        local(ids_ref, ids_buf, in_sem.at[2]),
        local(head_ref, head_buf, in_sem.at[3]),
    )
    for load in loads:
        load.start()

    def chunk_of(ref, side, k, by_rows):
        at = pl.ds(pl.multiple_of(side * half + k * WIDE, WIDE), WIDE)
        return ref.at[at, :] if by_rows else ref.at[:, at]

    def weight_side(buf, k, by_rows):
        return buf.at[k, :, side_of(core)] if by_rows else buf.at[k, side_of(core), :]

    weights = ((gate_ref, w_gate, False), (up_ref, w_up, False), (down_ref, w_down, True))

    def own_weight(k, a):
        ref, buf, by_rows = weights[a]
        return local(chunk_of(ref, core, k, by_rows), weight_side(buf, k, by_rows), own_sem.at[k, a])

    def sent_weight(k, a):
        ref, buf, by_rows = weights[a]
        return remote(
            chunk_of(ref, mate, k, by_rows), weight_side(buf, k, by_rows), w_send.at[k, a], w_recv.at[k, a], peer_core
        )

    def start_weights(make):
        for arrays in ((0, 1), (2,)):
            def step(k, carry, arrays=arrays):
                for a in arrays:
                    make(k, a).start()
                return carry

            lax.fori_loop(0, chunks, step, 0)

    start_weights(own_weight)
    pl.semaphore_wait(barrier, 7)

    blocks = {
        "own": row, "mate": z * 2 + 1 - xh,
        "up": up_z * 2 + xh, "up_m": up_z * 2 + 1 - xh,
        "dn": dn_z * 2 + xh, "dn_m": dn_z * 2 + 1 - xh,
        "far": ((z + 2) % 4) * 2 + xh, "far_m": ((z + 2) % 4) * 2 + 1 - xh,
    }
    peers = {"xh": peer_xh, "up": peer_up, "dn": peer_dn}

    def gather_send(t, m):
        here, there, peer = MESSAGES[m]
        return remote(
            rows_in.at[t, held(here), side_of(core)], rows_in.at[t, held(there), side_of(core)],
            x_send.at[t, m], x_recv.at[t, m], peers[peer],
        )

    def to_core(t, m, side=core):
        ref = rows_in.at[t, held("own" if m == 7 else MESSAGES[m][1]), side_of(side)]
        return remote(ref, ref, c_send.at[t, m], c_recv.at[t, m], peer_core)

    def pass_on(t, m, *then):
        gather_send(t, m).wait_recv()
        for n in then:
            gather_send(t, n).start()
        to_core(t, m).start()

    def from_core(t, *ms):
        for m in ms:
            to_core(t, m, mate).wait_recv()

    loads[0].wait()
    for m in (0, 1, 2):
        gather_send(0, m).start()
    to_core(0, 7).start()
    start_weights(sent_weight)

    for load in loads[1:]:
        load.wait()
    codes = logit_buf.shape[1]
    step_rows = 16

    def logit_step(i, carry):
        at = pl.ds(pl.multiple_of(i * step_rows, step_rows), step_rows)
        ids = ids_buf[at, :]
        code = lax.broadcasted_iota(jnp.int32, (step_rows, codes), 1)
        hit = ids[:, 0:1] == code
        for label in range(1, ids.shape[1]):
            hit = jnp.logical_or(hit, ids[:, label : label + 1] == code)
        target = jnp.where(hit, 1.0, 0.0)
        logit_grad[at, :] = (jax.nn.sigmoid(logit_buf[at, :]) - target).astype(BF16)
        return carry

    lax.fori_loop(0, block // step_rows, logit_step, 0)
    rows_in[1, held("own"), side_of(core)] = jnp.dot(
        logit_grad[...], head_buf[...], preferred_element_type=F32
    ).astype(BF16)
    for m in (0, 1, 2):
        gather_send(1, m).start()
    to_core(1, 7).start()

    total[...] = jnp.zeros_like(total)

    def peer_of(dim):
        return (row, jnp.where(dim == 0, col_x, jnp.where(dim == 1, col_1, col_2)))

    def turn(k, a):
        return (k + a) % 3

    def slot_of(k, a, b):
        r = turn(k, a)
        bits = ((b // 4 + x) % 2, (b // 2 + g1) % 2, (b + b // 2 + g2) % 2)
        slot = 0
        for dim, bit in enumerate(bits):
            e = (dim - r + 3) % 3
            slot = slot + bit * (4 - 2 * e + e * (e - 1) // 2)
        return slot

    def sum_send(step, k, a):
        size = (4, 2, 1)[step] * block
        dst = (land1, land2, land3)[step]
        return remote(
            part.at[k, a, pl.ds(size, size)], dst.at[k, a], s_send.at[step, k, a], s_recv.at[step, k, a],
            peer_of((turn(k, a) + step) % 3),
        )

    def give_send(step, k, a):
        size = (4, 2, 1)[step] * block
        return remote(
            delta.at[k, a, pl.ds(0, size)], delta.at[k, a, pl.ds(size, size)], g_send.at[step, k, a], g_recv.at[step, k, a],
            peer_of((turn(k, a) + step) % 3),
        )

    def got_weight(k, a):
        own_weight(k, a).wait()
        sent_weight(k, a).wait_recv()

    def forward_in(first, count, wait=False):
        def step(k, carry):
            for a, buf in ((0, w_gate), (1, w_up)):
                if wait:
                    got_weight(k, a)
                rows = rows_in[0, first * block : (first + count) * block, :]
                value = jnp.dot(rows, buf[k], preferred_element_type=F32).astype(BF16)
                for j in range(count):
                    slot = slot_of(k, a, blocks[ORDER[first + j]])
                    part[k, a, span(slot), :] = value[j * block : (j + 1) * block]

                    @pl.when(slot >= 4)
                    def _():
                        remote(
                            part.at[k, a, span(slot)], land1.at[k, a, span(slot - 4)],
                            s_send.at[0, k, a], s_recv.at[0, k, a], peer_of(turn(k, a)),
                        ).start()

            return carry

        return step

    def forward_out(k):
        got_weight(k, 2)
        value = lax.dot_general(rows_in[1], w_down[k], NT, preferred_element_type=F32).astype(BF16)
        for j, name in enumerate(ORDER):
            part[k, 2, span(slot_of(k, 2, blocks[name])), :] = value[j * block : (j + 1) * block]
        sum_send(0, k, 2).start()

    middle = (chunks + 1) // 2
    from_core(0, 7)
    lax.fori_loop(0, middle, forward_in(0, 1, True), 0)
    pass_on(0, 2, 6)
    pass_on(0, 1)
    pass_on(0, 0, 3, 4)
    lax.fori_loop(middle, chunks, forward_in(0, 1, True), 0)
    from_core(0, 1, 2)
    lax.fori_loop(0, chunks, forward_in(1, 2), 0)
    pass_on(0, 3, 5)
    pass_on(0, 6)
    pass_on(1, 2, 6)
    pass_on(1, 1)
    pass_on(1, 0, 3, 4)
    from_core(0, 0, 6)
    lax.fori_loop(0, chunks, forward_in(3, 2), 0)
    pass_on(0, 4)
    pass_on(0, 5)
    pass_on(1, 3, 5)
    pass_on(1, 6)
    from_core(0, 3, 4, 5)
    lax.fori_loop(0, chunks, forward_in(5, 3), 0)
    pass_on(1, 4)
    pass_on(1, 5)
    from_core(1, *range(8))
    forward_out(0)

    def add_in(k, a, land, first, count):
        for b in range(first, first + count):
            at = pl.ds(b * block, block)
            part[k, a, at, :] = part[k, a, at, :] + land[k, a, at, :]

    def sum_stage(step, k):
        land = (land1, land2)[step]
        keep = (2, 1)[step]
        for a in range(3):
            sum_send(step, k, a).wait_recv()
            add_in(k, a, land, keep, keep)
            sum_send(step + 1, k, a).start()
            add_in(k, a, land, 0, keep)

    def activate(k):
        for a in range(3):
            sum_send(2, k, a).wait_recv()
        piece = 32

        def act_step(i, carry):
            at = pl.ds(pl.multiple_of(i * piece, piece), piece)
            gate, upper, back = (part[k, a, at, :].astype(F32) + land3[k, a, at, :].astype(F32) for a in range(3))
            sig = jax.nn.sigmoid(gate)
            silu = gate * sig
            delta[k, 0, at, :] = (back * upper * sig * (1.0 + gate * (1.0 - sig))).astype(BF16)
            delta[k, 1, at, :] = (back * silu).astype(BF16)
            delta[k, 2, at, :] = (silu * upper).astype(BF16)
            return carry

        lax.fori_loop(0, block // piece, act_step, 0)
        for a in range(3):
            give_send(2, k, a).start()

    def give_stage(step, k, arrays=(0, 1)):
        for a in arrays:
            give_send(step, k, a).wait_recv()
            give_send(step - 1, k, a).start()

    outs = (out_g, out_u, out_h)

    def own_out(k, a):
        src = hidden_turned.at[k] if a == 2 else part.at[k, a]
        return local(src, chunk_of(outs[a], core, k, a == 2), o_local.at[k, a])

    def core_out(k, a, side=core):
        src = hidden_turned.at[k] if a == 2 else part.at[k, a]
        return remote(src, chunk_of(outs[a], side, k, a == 2), o_send.at[k, a], o_recv.at[k, a], peer_core)

    def finish(k, a):
        give_send(0, k, a).wait_recv()
        for step in range(3):
            sum_send(step, k, a).wait_send()
        for name in ORDER:
            part[k, a, held(name), :] = delta[k, a, span(slot_of(k, a, blocks[name])), :]
        if a == 2:
            tokens = 8 * block
            for at in range(0, tokens, 128):
                hidden_turned[k, :, at : at + 128] = part[k, 2, at : at + 128, :].T
        own_out(k, a).start()
        core_out(k, a).start()

    def backward(k):
        for a in range(2):
            finish(k, a)
        total[...] = (
            total[...]
            + lax.dot_general(part[k, 0], w_gate[k], NT, preferred_element_type=F32)
            + lax.dot_general(part[k, 1], w_up[k], NT, preferred_element_type=F32)
        )

    grad_copy = local(rows_in.at[1, :, side_of(core)], grad_all, xo_sem.at[0])
    turned_copy = local(turned, acts_turned, xo_sem.at[1])

    def turn_inputs():
        grad_copy.start()
        for at in range(0, feats, 128):
            column = pl.ds(pl.multiple_of(core * feats + at, 128), 128)
            turned[at : at + 128, :] = rows_in[0, :, column].T
        turned_copy.start()

    def late_give(first, last):
        def step(k, carry):
            give_stage(1, k, (2,))
            return carry

        lax.fori_loop(min(first, chunks), min(last, chunks), step, 0)

    def slot_step(i, carry):
        @pl.when(i + 1 < chunks)
        def _():
            forward_out(i + 1)

        def stage(lag, run):
            @pl.when(jnp.logical_and(i >= lag, i < chunks + lag))
            def _():
                run(i - lag)

        stage(0, functools.partial(sum_stage, 0))
        stage(1, functools.partial(sum_stage, 1))
        stage(2, activate)
        stage(3, functools.partial(give_stage, 2))
        stage(4, functools.partial(give_stage, 1))
        stage(5, backward)

        @pl.when(i == 0)
        def _():
            turn_inputs()

        @pl.when(i >= chunks)
        def _():
            first = 2 * (i - chunks)
            for k in (first, first + 1):
                @pl.when(k < chunks)
                def _():
                    give_stage(2, k, (2,))

        @pl.when(i == chunks + 3)
        def _():
            late_give(0, 3)

        return carry

    lax.fori_loop(0, chunks + 5, slot_step, 0)

    def late_finish(first, last):
        def step(k, carry):
            finish(k, 2)
            return carry

        lax.fori_loop(min(first, chunks), min(last, chunks), step, 0)

    cored = ("far", "far_m", "up_m", "dn", "up", "dn_m", "mate", "own")

    def core_sum(n):
        at = held(cored[n])
        return remote(mate_send.at[at], mate_land.at[at], t_send.at[7 + n], t_recv.at[7 + n], peer_core)

    for n, name in enumerate(cored):
        mate_send[held(name), :] = total[held(name), side_of(mate)].astype(BF16)
        core_sum(n).start()

    def core_add(n):
        core_sum(n).wait_recv()
        at = held(cored[n])
        both = total[at, side_of(core)] + mate_land[at, :].astype(F32)
        if n < 4:
            side_send[at, :] = both.astype(BF16)
        else:
            total[at, side_of(core)] = both

    def mine(name):
        return total[held(name), side_of(core)]

    def send_block(m, name, peer):
        return remote(side_send.at[held(name)], side_land.at[m], t_send.at[m], t_recv.at[m], peer)

    far_up = send_block(0, "far", peer_up)
    far_dn = send_block(1, "far_m", peer_dn)
    one_up = send_block(2, "up_m", peer_up)
    one_dn = send_block(3, "dn", peer_dn)
    two_up = send_block(4, "up", peer_up)
    two_dn = send_block(5, "dn_m", peer_dn)
    swap = send_block(6, "mate", peer_xh)
    core_add(0)
    far_up.start()
    core_add(1)
    far_dn.start()
    core_add(2)
    one_up.start()
    core_add(3)
    one_dn.start()
    for n in range(4, 8):
        core_add(n)
    late_give(3, 5)
    far_up.wait_recv()
    side_send[held("up"), :] = (mine("up") + side_land[0].astype(F32)).astype(BF16)
    two_up.start()
    far_dn.wait_recv()
    side_send[held("dn_m"), :] = (mine("dn_m") + side_land[1].astype(F32)).astype(BF16)
    two_dn.start()
    late_give(5, chunks)
    late_finish(0, 1)
    one_up.wait_recv()
    two_dn.wait_recv()
    side_send[held("mate"), :] = (mine("mate") + side_land[2].astype(F32) + side_land[5].astype(F32)).astype(BF16)
    swap.start()
    late_finish(1, chunks - 1)
    one_dn.wait_recv()
    two_up.wait_recv()
    kept = mine("own") + side_land[3].astype(F32) + side_land[4].astype(F32)
    swap.wait_recv()
    side_send[held("own"), :] = (kept + side_land[6].astype(F32)).astype(BF16)
    result = local(side_send.at[held("own")], acts_grad, xo_sem.at[2])
    result.start()
    late_finish(chunks - 1, chunks)

    def drain(k, carry):
        for a in range(3):
            sent_weight(k, a).wait_send()
            own_out(k, a).wait()
            core_out(k, a).wait_send()
            core_out(k, a, mate).wait_recv()
            for step in range(3):
                give_send(step, k, a).wait_send()
        return carry

    lax.fori_loop(0, chunks, drain, 0)
    for t in range(2):
        for m in range(7):
            gather_send(t, m).wait_send()
        for m in range(8):
            to_core(t, m).wait_send()
    grad_copy.wait()
    turned_copy.wait()
    for n in range(8):
        core_sum(n).wait_send()
    for copy in (far_up, far_dn, one_up, one_dn, two_up, two_dn, swap):
        copy.wait_send()
    result.wait()


def grads_kernel(factor, turned, grad_all, gate_delta, up_delta, hidden, gate_grad, up_grad, down_grad):
    gate_grad[...] = (jnp.dot(turned[...], gate_delta[...], preferred_element_type=F32) * factor).astype(BF16)
    up_grad[...] = (jnp.dot(turned[...], up_delta[...], preferred_element_type=F32) * factor).astype(BF16)
    down_grad[...] = (jnp.dot(hidden[...], grad_all[...], preferred_element_type=F32) * factor).astype(BF16)


def weight_grads(turned, grad_all, gate_delta, up_delta, hidden):
    (feats, tokens), width = turned.shape, hidden.shape[0]
    step = 2 * WIDE
    columns = pl.BlockSpec((feats, step), lambda i: (0, i))
    return pl.pallas_call(
        functools.partial(grads_kernel, 1.0 / tokens**0.5),
        grid=(width // step,),
        out_shape=(
            jax.ShapeDtypeStruct((feats, width), BF16), jax.ShapeDtypeStruct((feats, width), BF16),
            jax.ShapeDtypeStruct((width, feats), BF16),
        ),
        in_specs=[
            pl.BlockSpec((feats, tokens), lambda i: (0, 0)),
            pl.BlockSpec((tokens, feats), lambda i: (0, 0)),
            pl.BlockSpec((tokens, step), lambda i: (0, i)),
            pl.BlockSpec((tokens, step), lambda i: (0, i)),
            pl.BlockSpec((step, tokens), lambda i: (i, 0)),
        ],
        out_specs=(columns, columns, pl.BlockSpec((step, feats), lambda i: (i, 0))),
        compiler_params=pltpu.CompilerParams(vmem_limit_bytes=48 * 2**20),
        cost_estimate=pl.CostEstimate(
            flops=6 * tokens * feats * width, bytes_accessed=6 * (tokens + feats) * width, transcendentals=0
        ),
        name="grads_kernel",
    )(turned, grad_all, gate_delta, up_delta, hidden)


def per_device(acts, logits, label_ids, head_weight, gate_weight, up_weight, down_weight):
    tokens = acts.shape[0] * 8
    width, feats = gate_weight.shape[1], acts.shape[1]
    block = acts.shape[0]
    chunks = width // 2 // WIDE
    any_spec = pl.BlockSpec(memory_space=pl.ANY)
    dma = pltpu.SemaphoreType.DMA
    hidden_shape = jax.ShapeDtypeStruct((tokens, width), BF16)
    rows_shape = jax.ShapeDtypeStruct((tokens, feats), BF16)
    turned, grad_all, hidden, gate_delta, up_delta, acts_grad = pl.pallas_call(
        functools.partial(layer_kernel, chunks),
        out_shape=(
            jax.ShapeDtypeStruct((feats, tokens), BF16), rows_shape, jax.ShapeDtypeStruct((width, tokens), BF16),
            hidden_shape, hidden_shape, jax.ShapeDtypeStruct(acts.shape, BF16),
        ),
        in_specs=[any_spec] * 7,
        out_specs=(any_spec,) * 6,
        scratch_shapes=[
            pltpu.VMEM((2, tokens, 2 * feats), BF16),
            pltpu.VMEM((chunks, 2 * feats, WIDE), BF16),
            pltpu.VMEM((chunks, 2 * feats, WIDE), BF16),
            pltpu.VMEM((chunks, WIDE, 2 * feats), BF16),
            pltpu.VMEM((chunks, 3, tokens, WIDE), BF16),
            pltpu.VMEM((chunks, 3, 4 * block, WIDE), BF16),
            pltpu.VMEM((chunks, 3, 2 * block, WIDE), BF16),
            pltpu.VMEM((chunks, 3, block, WIDE), BF16),
            pltpu.VMEM((chunks, 3, tokens, WIDE), BF16),
            pltpu.VMEM((tokens, 2 * feats), F32),
            pltpu.VMEM(logits.shape, F32),
            pltpu.VMEM(label_ids.shape, jnp.int32),
            pltpu.VMEM(head_weight.shape, BF16),
            pltpu.VMEM(logits.shape, BF16),
            pltpu.VMEM((feats, tokens), BF16),
            pltpu.VMEM((chunks, WIDE, tokens), BF16),
            pltpu.VMEM((tokens, feats), BF16),
            pltpu.VMEM((tokens, feats), BF16),
            pltpu.VMEM((tokens, feats), BF16),
            pltpu.VMEM((7, block, feats), BF16),
            dma((4,)), dma((chunks, 3)), dma((chunks, 3)), dma((chunks, 3)),
            dma((2, 7)), dma((2, 7)), dma((2, 8)), dma((2, 8)),
            dma((3, chunks, 3)), dma((3, chunks, 3)), dma((3, chunks, 3)), dma((3, chunks, 3)),
            dma((chunks, 3)), dma((chunks, 3)), dma((chunks, 3)), dma((15,)), dma((15,)), dma((3,)),
        ],
        compiler_params=pltpu.CompilerParams(collective_id=0, has_side_effects=True, vmem_limit_bytes=60 * 2**20),
        name="layer_kernel",
    )(acts, logits, label_ids, head_weight, gate_weight, up_weight, down_weight)
    gate_grad, up_grad, down_grad = weight_grads(turned, grad_all, gate_delta, up_delta, hidden)
    return acts_grad, gate_grad, up_grad, down_grad


def solution(mesh):
    placed = (
        P("row", "col"),
        P("row", None),
        P("row", None),
        P(None, "col"),
        P("col", "row"),
        P("col", "row"),
        P("row", "col"),
    )
    return jax.shard_map(
        per_device,
        mesh=mesh,
        in_specs=placed,
        out_specs=(P("row", "col"), P("col", "row"), P("col", "row"), P("row", "col")),
        check_vma=False,
    )
```

```python
import functools

import jax
import jax.numpy as jnp
from jax import lax
from jax.experimental import pallas as pl
from jax.experimental.pallas import tpu as pltpu
from jax.sharding import PartitionSpec as P

MESH = pl.DeviceIdType.MESH
BF16 = jnp.bfloat16
F32 = jnp.float32
WIDE = 256
NT = (((1,), (1,)), ((), ()))
ORDER = ("own", "up", "dn", "mate", "far", "up_m", "dn_m", "far_m")
MESSAGES = (
    ("own", "mate", "xh"),
    ("own", "dn", "up"),
    ("own", "up", "dn"),
    ("mate", "dn_m", "up"),
    ("mate", "up_m", "dn"),
    ("dn_m", "far_m", "up"),
    ("up", "far", "dn"),
)


def layer_kernel(
    chunks,
    acts_ref, logits_ref, ids_ref, head_ref, gate_ref, up_ref, down_ref,
    acts_turned, grad_all, out_h, out_g, out_u, kept_out, mate_out,
    rows_in, w_gate, w_up, w_down, part, land1, land2, land3, delta,
    total, logit_buf, ids_buf, ids_turned, head_buf, logit_grad, turned, hidden_turned,
    mate_send, mate_land, side_send, side_land,
    in_sem, own_sem, w_send, w_recv, x_send, x_recv, c_send, c_recv,
    s_send, s_recv, g_send, g_recv, o_local, o_send, o_recv, t_send, t_recv, xo_sem,
):
    row, col = lax.axis_index("row"), lax.axis_index("col")
    z, xh = row // 2, row % 2
    core, y, x = col % 2, (col // 2) % 4, col // 8
    g1, g2 = (y % 2 + y // 2) % 2, y // 2
    block = acts_ref.shape[0]
    half = chunks * WIDE
    feats = acts_ref.shape[1]
    mate = 1 - core
    col_x = col + 8 - 16 * x
    col_1 = x * 8 + (y + 1 - 2 * (y % 2)) * 2 + core
    col_2 = x * 8 + ((y + 3 + 2 * (y % 2)) % 4) * 2 + core
    up_z, dn_z = (z + 1) % 4, (z + 3) % 4
    peer_core = (row, col + 1 - 2 * core)
    peer_xh = (z * 2 + 1 - xh, col)
    peer_up = (up_z * 2 + xh, col)
    peer_dn = (dn_z * 2 + xh, col)

    barrier = pltpu.get_barrier_semaphore()
    for peer in (peer_core, peer_xh, peer_up, peer_dn, (row, col_x), (row, col_1), (row, col_2)):
        pl.semaphore_signal(barrier, inc=1, device_id=peer, device_id_type=MESH)

    def local(src, dst, sem):
        return pltpu.make_async_copy(src, dst, sem)

    def remote(src, dst, ssem, rsem, peer):
        return pltpu.make_async_remote_copy(
            src_ref=src, dst_ref=dst, send_sem=ssem, recv_sem=rsem, device_id=peer, device_id_type=MESH
        )

    def span(index):
        return pl.ds(pl.multiple_of(index * block, block), block)

    def held(name):
        return pl.ds(ORDER.index(name) * block, block)

    def side_of(index):
        return pl.ds(pl.multiple_of(index * feats, feats), feats)

    loads = (
        local(acts_ref, rows_in.at[0, held("own"), side_of(core)], in_sem.at[0]),
        local(logits_ref, logit_buf, in_sem.at[1]),
        local(ids_ref, ids_buf, in_sem.at[2]),
        local(head_ref, head_buf, in_sem.at[3]),
    )
    for load in loads:
        load.start()

    def chunk_of(ref, side, k, by_rows):
        at = pl.ds(pl.multiple_of(side * half + k * WIDE, WIDE), WIDE)
        return ref.at[at, :] if by_rows else ref.at[:, at]

    def weight_side(buf, k, by_rows):
        return buf.at[k, :, side_of(core)] if by_rows else buf.at[k, side_of(core), :]

    weights = ((gate_ref, w_gate, False), (up_ref, w_up, False), (down_ref, w_down, True))

    def own_weight(k, a):
        ref, buf, by_rows = weights[a]
        return local(chunk_of(ref, core, k, by_rows), weight_side(buf, k, by_rows), own_sem.at[k, a])

    def sent_weight(k, a):
        ref, buf, by_rows = weights[a]
        return remote(
            chunk_of(ref, mate, k, by_rows), weight_side(buf, k, by_rows), w_send.at[k, a], w_recv.at[k, a], peer_core
        )

    def start_weights(make):
        for arrays in ((0, 1), (2,)):
            def step(k, carry, arrays=arrays):
                for a in arrays:
                    make(k, a).start()
                return carry

            lax.fori_loop(0, chunks, step, 0)

    start_weights(own_weight)
    pl.semaphore_wait(barrier, 7)

    blocks = {
        "own": row, "mate": z * 2 + 1 - xh,
        "up": up_z * 2 + xh, "up_m": up_z * 2 + 1 - xh,
        "dn": dn_z * 2 + xh, "dn_m": dn_z * 2 + 1 - xh,
        "far": ((z + 2) % 4) * 2 + xh, "far_m": ((z + 2) % 4) * 2 + 1 - xh,
    }
    peers = {"xh": peer_xh, "up": peer_up, "dn": peer_dn}

    def gather_send(t, m):
        here, there, peer = MESSAGES[m]
        return remote(
            rows_in.at[t, held(here), side_of(core)], rows_in.at[t, held(there), side_of(core)],
            x_send.at[t, m], x_recv.at[t, m], peers[peer],
        )

    def to_core(t, m, side=core):
        ref = rows_in.at[t, held("own" if m == 7 else MESSAGES[m][1]), side_of(side)]
        return remote(ref, ref, c_send.at[t, m], c_recv.at[t, m], peer_core)

    def pass_on(t, m, *then):
        gather_send(t, m).wait_recv()
        for n in then:
            gather_send(t, n).start()
        to_core(t, m).start()

    def from_core(t, *ms):
        for m in ms:
            to_core(t, m, mate).wait_recv()

    loads[0].wait()
    for m in (0, 1, 2):
        gather_send(0, m).start()
    to_core(0, 7).start()
    start_weights(sent_weight)

    for load in loads[1:]:
        load.wait()
    ids_turned[...] = ids_buf[...].T
    codes = logit_buf.shape[1]
    step_rows = 16

    def logit_step(i, carry):
        at = pl.ds(pl.multiple_of(i * step_rows, step_rows), step_rows)
        ids = ids_turned[at, :]
        code = lax.broadcasted_iota(jnp.int32, (step_rows, codes), 1)
        hit = ids[:, 0:1] == code
        for label in range(1, ids.shape[1]):
            hit = jnp.logical_or(hit, ids[:, label : label + 1] == code)
        target = jnp.where(hit, 1.0, 0.0)
        logit_grad[at, :] = (jax.nn.sigmoid(logit_buf[at, :]) - target).astype(BF16)
        return carry

    lax.fori_loop(0, block // step_rows, logit_step, 0)
    rows_in[1, held("own"), side_of(core)] = jnp.dot(
        logit_grad[...], head_buf[...], preferred_element_type=F32
    ).astype(BF16)
    total[...] = jnp.zeros_like(total)
    gather_send(0, 2).wait_recv()
    gather_send(0, 6).start()
    for m in (0, 1, 2):
        gather_send(1, m).start()
    gather_send(0, 0).wait_recv()
    for m in (3, 4):
        gather_send(0, m).start()
    gather_send(0, 1).wait_recv()
    for m in (1, 2, 0):
        to_core(0, m).start()
    to_core(1, 7).start()

    def peer_of(dim):
        return (row, jnp.where(dim == 0, col_x, jnp.where(dim == 1, col_1, col_2)))

    def turn(k, a):
        return (k + a) % 3

    def slot_of(k, a, b):
        r = turn(k, a)
        bits = ((b // 4 + x) % 2, (b // 2 + g1) % 2, (b + b // 2 + g2) % 2)
        slot = 0
        for dim, bit in enumerate(bits):
            e = (dim - r + 3) % 3
            slot = slot + bit * (4 - 2 * e + e * (e - 1) // 2)
        return slot

    def sum_send(step, k, a):
        size = (4, 2, 1)[step] * block
        dst = (land1, land2, land3)[step]
        return remote(
            part.at[k, a, pl.ds(size, size)], dst.at[k, a], s_send.at[step, k, a], s_recv.at[step, k, a],
            peer_of((turn(k, a) + step) % 3),
        )

    def give_send(step, k, a):
        size = (4, 2, 1)[step] * block
        return remote(
            delta.at[k, a, pl.ds(0, size)], delta.at[k, a, pl.ds(size, size)], g_send.at[step, k, a], g_recv.at[step, k, a],
            peer_of((turn(k, a) + step) % 3),
        )

    def got_weight(k, a):
        own_weight(k, a).wait()
        sent_weight(k, a).wait_recv()

    def forward_in(first, count, wait=False):
        def step(k, carry):
            for a, buf in ((0, w_gate), (1, w_up)):
                if wait:
                    got_weight(k, a)
                rows = rows_in[0, first * block : (first + count) * block, :]
                value = jnp.dot(rows, buf[k], preferred_element_type=F32).astype(BF16)
                for j in range(count):
                    slot = slot_of(k, a, blocks[ORDER[first + j]])
                    part[k, a, span(slot), :] = value[j * block : (j + 1) * block]

                    @pl.when(slot >= 4)
                    def _():
                        remote(
                            part.at[k, a, span(slot)], land1.at[k, a, span(slot - 4)],
                            s_send.at[0, k, a], s_recv.at[0, k, a], peer_of(turn(k, a)),
                        ).start()

            return carry

        return step

    def forward_out(k):
        got_weight(k, 2)
        value = lax.dot_general(rows_in[1], w_down[k], NT, preferred_element_type=F32).astype(BF16)
        for j, name in enumerate(ORDER):
            part[k, 2, span(slot_of(k, 2, blocks[name])), :] = value[j * block : (j + 1) * block]
        sum_send(0, k, 2).start()

    from_core(0, 7, 1, 2)
    lax.fori_loop(0, chunks, forward_in(0, 3, True), 0)
    pass_on(0, 3, 5)
    pass_on(0, 6)
    pass_on(0, 4)
    pass_on(1, 2, 6)
    pass_on(1, 1)
    pass_on(1, 0, 3, 4)
    from_core(0, 0, 3, 4, 6)
    lax.fori_loop(0, chunks, forward_in(3, 4), 0)
    pass_on(0, 5)
    pass_on(1, 3, 5)
    pass_on(1, 6)
    pass_on(1, 4)
    from_core(0, 5)
    lax.fori_loop(0, chunks, forward_in(7, 1), 0)
    pass_on(1, 5)
    from_core(1, *range(8))
    forward_out(0)

    def add_in(k, a, land, first, count):
        for b in range(first, first + count):
            at = pl.ds(b * block, block)
            part[k, a, at, :] = part[k, a, at, :] + land[k, a, at, :]

    def sum_stage(step, k):
        land = (land1, land2)[step]
        keep = (2, 1)[step]
        for a in range(3):
            sum_send(step, k, a).wait_recv()
            add_in(k, a, land, keep, keep)
            sum_send(step + 1, k, a).start()
            add_in(k, a, land, 0, keep)

    def activate(k):
        for a in range(3):
            sum_send(2, k, a).wait_recv()
        piece = 32

        def act_step(i, carry):
            at = pl.ds(pl.multiple_of(i * piece, piece), piece)
            gate, upper, back = (part[k, a, at, :].astype(F32) + land3[k, a, at, :].astype(F32) for a in range(3))
            sig = jax.nn.sigmoid(gate)
            silu = gate * sig
            delta[k, 0, at, :] = (back * upper * sig * (1.0 + gate * (1.0 - sig))).astype(BF16)
            delta[k, 1, at, :] = (back * silu).astype(BF16)
            delta[k, 2, at, :] = (silu * upper).astype(BF16)
            return carry

        lax.fori_loop(0, block // piece, act_step, 0)
        for a in range(3):
            give_send(2, k, a).start()

    def give_stage(step, k, arrays=(0, 1)):
        for a in arrays:
            give_send(step, k, a).wait_recv()
            give_send(step - 1, k, a).start()

    outs = (out_g, out_u, out_h)

    def own_out(k, a):
        src = hidden_turned.at[k] if a == 2 else part.at[k, a]
        return local(src, chunk_of(outs[a], core, k, a == 2), o_local.at[k, a])

    def core_out(k, a, side=core):
        src = hidden_turned.at[k] if a == 2 else part.at[k, a]
        return remote(src, chunk_of(outs[a], side, k, a == 2), o_send.at[k, a], o_recv.at[k, a], peer_core)

    def finish(k, a):
        give_send(0, k, a).wait_recv()
        for step in range(3):
            sum_send(step, k, a).wait_send()
        for name in ORDER:
            part[k, a, held(name), :] = delta[k, a, span(slot_of(k, a, blocks[name])), :]
        if a == 2:
            tokens = 8 * block
            for at in range(0, tokens, 128):
                hidden_turned[k, :, at : at + 128] = part[k, 2, at : at + 128, :].T
        own_out(k, a).start()
        core_out(k, a).start()

    def backward(k):
        for a in range(2):
            finish(k, a)
        total[...] = (
            total[...]
            + lax.dot_general(part[k, 0], w_gate[k], NT, preferred_element_type=F32)
            + lax.dot_general(part[k, 1], w_up[k], NT, preferred_element_type=F32)
        )

    grad_copy = local(rows_in.at[1, :, side_of(core)], grad_all, xo_sem.at[0])
    turned_copy = local(turned, acts_turned, xo_sem.at[1])

    def turn_inputs():
        grad_copy.start()
        for at in range(0, feats, 128):
            column = pl.ds(pl.multiple_of(core * feats + at, 128), 128)
            turned[at : at + 128, :] = rows_in[0, :, column].T
        turned_copy.start()

    def late_give(first, last):
        def step(k, carry):
            give_stage(1, k, (2,))
            return carry

        lax.fori_loop(min(first, chunks), min(last, chunks), step, 0)

    def slot_step(i, carry):
        @pl.when(i + 1 < chunks)
        def _():
            forward_out(i + 1)

        def stage(lag, run):
            @pl.when(jnp.logical_and(i >= lag, i < chunks + lag))
            def _():
                run(i - lag)

        stage(0, functools.partial(sum_stage, 0))
        stage(1, functools.partial(sum_stage, 1))
        stage(2, activate)
        stage(3, functools.partial(give_stage, 2))
        stage(4, functools.partial(give_stage, 1))
        stage(5, backward)

        @pl.when(i == 0)
        def _():
            turn_inputs()

        @pl.when(i >= chunks)
        def _():
            first = 2 * (i - chunks)
            for k in (first, first + 1):
                @pl.when(k < chunks)
                def _():
                    give_stage(2, k, (2,))

        @pl.when(i == chunks + 3)
        def _():
            late_give(0, 3)

        return carry

    lax.fori_loop(0, chunks + 5, slot_step, 0)

    def late_finish(first, last):
        def step(k, carry):
            finish(k, 2)
            return carry

        lax.fori_loop(min(first, chunks), min(last, chunks), step, 0)

    cored = ("far", "far_m", "up_m", "dn", "up", "dn_m", "mate", "own")

    def core_sum(n):
        at = held(cored[n])
        return remote(mate_send.at[at], mate_land.at[at], t_send.at[7 + n], t_recv.at[7 + n], peer_core)

    for n, name in enumerate(cored):
        mate_send[held(name), :] = total[held(name), side_of(mate)].astype(BF16)
        core_sum(n).start()

    def core_add(n):
        core_sum(n).wait_recv()
        at = held(cored[n])
        both = total[at, side_of(core)] + mate_land[at, :].astype(F32)
        if n < 4:
            side_send[at, :] = both.astype(BF16)
        else:
            total[at, side_of(core)] = both

    def mine(name):
        return total[held(name), side_of(core)]

    def send_block(m, name, peer):
        return remote(side_send.at[held(name)], side_land.at[m], t_send.at[m], t_recv.at[m], peer)

    far_up = send_block(0, "far", peer_up)
    far_dn = send_block(1, "far_m", peer_dn)
    one_up = send_block(2, "up_m", peer_up)
    one_dn = send_block(3, "dn", peer_dn)
    two_up = send_block(4, "up", peer_up)
    two_dn = send_block(5, "dn_m", peer_dn)
    core_add(0)
    far_up.start()
    core_add(1)
    far_dn.start()
    core_add(2)
    one_up.start()
    core_add(3)
    one_dn.start()
    for n in range(4, 8):
        core_add(n)
    late_give(3, 5)
    far_up.wait_recv()
    side_send[held("up"), :] = (mine("up") + side_land[0].astype(F32)).astype(BF16)
    two_up.start()
    far_dn.wait_recv()
    side_send[held("dn_m"), :] = (mine("dn_m") + side_land[1].astype(F32)).astype(BF16)
    two_dn.start()
    late_give(5, chunks)
    late_finish(0, 1)
    one_up.wait_recv()
    two_dn.wait_recv()
    side_send[held("mate"), :] = (mine("mate") + side_land[2].astype(F32) + side_land[5].astype(F32)).astype(BF16)
    one_dn.wait_recv()
    two_up.wait_recv()
    total[held("own"), side_of(core)] = mine("own") + side_land[3].astype(F32) + side_land[4].astype(F32)
    results = (
        local(side_send.at[held("mate")], mate_out, xo_sem.at[2]),
        local(total.at[held("own"), side_of(core)], kept_out, xo_sem.at[3]),
    )
    for copy in results:
        copy.start()
    late_finish(1, chunks)

    def drain(k, carry):
        for a in range(3):
            sent_weight(k, a).wait_send()
            own_out(k, a).wait()
            core_out(k, a).wait_send()
            core_out(k, a, mate).wait_recv()
            for step in range(3):
                give_send(step, k, a).wait_send()
        return carry

    lax.fori_loop(0, chunks, drain, 0)
    for t in range(2):
        for m in range(7):
            gather_send(t, m).wait_send()
        for m in range(8):
            to_core(t, m).wait_send()
    grad_copy.wait()
    turned_copy.wait()
    for n in range(8):
        core_sum(n).wait_send()
    for copy in (far_up, far_dn, one_up, one_dn, two_up, two_dn):
        copy.wait_send()
    for copy in results:
        copy.wait()


def grads_kernel(factor, turned, grad_all, gate_delta, up_delta, hidden, gate_grad, up_grad, down_grad):
    gate_grad[...] = (jnp.dot(turned[...], gate_delta[...], preferred_element_type=F32) * factor).astype(BF16)
    up_grad[...] = (jnp.dot(turned[...], up_delta[...], preferred_element_type=F32) * factor).astype(BF16)
    down_grad[...] = (jnp.dot(hidden[...], grad_all[...], preferred_element_type=F32) * factor).astype(BF16)


def weight_grads(turned, grad_all, gate_delta, up_delta, hidden):
    (feats, tokens), width = turned.shape, hidden.shape[0]
    step = width // 4
    columns = pl.BlockSpec((feats, step), lambda i: (0, i))
    return pl.pallas_call(
        functools.partial(grads_kernel, 1.0 / tokens**0.5),
        grid=(width // step,),
        out_shape=(
            jax.ShapeDtypeStruct((feats, width), BF16), jax.ShapeDtypeStruct((feats, width), BF16),
            jax.ShapeDtypeStruct((width, feats), BF16),
        ),
        in_specs=[
            pl.BlockSpec((feats, tokens), lambda i: (0, 0)),
            pl.BlockSpec((tokens, feats), lambda i: (0, 0)),
            pl.BlockSpec((tokens, step), lambda i: (0, i)),
            pl.BlockSpec((tokens, step), lambda i: (0, i)),
            pl.BlockSpec((step, tokens), lambda i: (i, 0)),
        ],
        out_specs=(columns, columns, pl.BlockSpec((step, feats), lambda i: (i, 0))),
        compiler_params=pltpu.CompilerParams(vmem_limit_bytes=48 * 2**20),
        cost_estimate=pl.CostEstimate(
            flops=6 * tokens * feats * width, bytes_accessed=6 * (tokens + feats) * width, transcendentals=0
        ),
        name="grads_kernel",
    )(turned, grad_all, gate_delta, up_delta, hidden)


def per_device(acts, logits, label_ids, head_weight, gate_weight, up_weight, down_weight):
    tokens = acts.shape[0] * 8
    width, feats = gate_weight.shape[1], acts.shape[1]
    block = acts.shape[0]
    chunks = width // 2 // WIDE
    any_spec = pl.BlockSpec(memory_space=pl.ANY)
    dma = pltpu.SemaphoreType.DMA
    hidden_shape = jax.ShapeDtypeStruct((tokens, width), BF16)
    rows_shape = jax.ShapeDtypeStruct((tokens, feats), BF16)
    turned, grad_all, hidden, gate_delta, up_delta, kept, passed = pl.pallas_call(
        functools.partial(layer_kernel, chunks),
        out_shape=(
            jax.ShapeDtypeStruct((feats, tokens), BF16), rows_shape, jax.ShapeDtypeStruct((width, tokens), BF16),
            hidden_shape, hidden_shape, jax.ShapeDtypeStruct(acts.shape, F32), jax.ShapeDtypeStruct(acts.shape, BF16),
        ),
        in_specs=[any_spec] * 7,
        out_specs=(any_spec,) * 7,
        scratch_shapes=[
            pltpu.VMEM((2, tokens, 2 * feats), BF16),
            pltpu.VMEM((chunks, 2 * feats, WIDE), BF16),
            pltpu.VMEM((chunks, 2 * feats, WIDE), BF16),
            pltpu.VMEM((chunks, WIDE, 2 * feats), BF16),
            pltpu.VMEM((chunks, 3, tokens, WIDE), BF16),
            pltpu.VMEM((chunks, 3, 4 * block, WIDE), BF16),
            pltpu.VMEM((chunks, 3, 2 * block, WIDE), BF16),
            pltpu.VMEM((chunks, 3, block, WIDE), BF16),
            pltpu.VMEM((chunks, 3, tokens, WIDE), BF16),
            pltpu.VMEM((tokens, 2 * feats), F32),
            pltpu.VMEM(logits.shape, F32),
            pltpu.VMEM(label_ids.shape[::-1], jnp.int32),
            pltpu.VMEM(label_ids.shape, jnp.int32),
            pltpu.VMEM(head_weight.shape, BF16),
            pltpu.VMEM(logits.shape, BF16),
            pltpu.VMEM((feats, tokens), BF16),
            pltpu.VMEM((chunks, WIDE, tokens), BF16),
            pltpu.VMEM((tokens, feats), BF16),
            pltpu.VMEM((tokens, feats), BF16),
            pltpu.VMEM((tokens, feats), BF16),
            pltpu.VMEM((6, block, feats), BF16),
            dma((4,)), dma((chunks, 3)), dma((chunks, 3)), dma((chunks, 3)),
            dma((2, 7)), dma((2, 7)), dma((2, 8)), dma((2, 8)),
            dma((3, chunks, 3)), dma((3, chunks, 3)), dma((3, chunks, 3)), dma((3, chunks, 3)),
            dma((chunks, 3)), dma((chunks, 3)), dma((chunks, 3)), dma((15,)), dma((15,)), dma((4,)),
        ],
        compiler_params=pltpu.CompilerParams(collective_id=0, has_side_effects=True, vmem_limit_bytes=60 * 2**20),
        name="layer_kernel",
    )(acts, logits, label_ids.T, head_weight, gate_weight, up_weight, down_weight)
    swapped = lax.ppermute(passed, "row", [(at, at + 1 - 2 * (at % 2)) for at in range(8)])
    acts_grad = (kept + swapped.astype(F32)).astype(BF16)
    gate_grad, up_grad, down_grad = weight_grads(turned, grad_all, gate_delta, up_delta, hidden)
    return acts_grad, gate_grad, up_grad, down_grad


def solution(mesh):
    placed = (
        P("row", "col"),
        P("row", None),
        P("row", None),
        P(None, "col"),
        P("col", "row"),
        P("col", "row"),
        P("row", "col"),
    )
    return jax.shard_map(
        per_device,
        mesh=mesh,
        in_specs=placed,
        out_specs=(P("row", "col"), P("col", "row"), P("col", "row"), P("row", "col")),
        check_vma=False,
    )
```

```python
import functools

import jax
import jax.numpy as jnp
from jax import lax
from jax.experimental import pallas as pl
from jax.experimental.pallas import tpu as pltpu
from jax.sharding import PartitionSpec as P

MESH = pl.DeviceIdType.MESH
BF16 = jnp.bfloat16
F32 = jnp.float32
WIDE = 256
NT = (((1,), (1,)), ((), ()))
ORDER = ("own", "up", "dn", "mate", "far", "up_m", "dn_m", "far_m")
MESSAGES = (
    ("own", "mate", "xh"),
    ("own", "dn", "up"),
    ("own", "up", "dn"),
    ("mate", "dn_m", "up"),
    ("mate", "up_m", "dn"),
    ("dn_m", "far_m", "up"),
    ("up", "far", "dn"),
)


def layer_kernel(
    chunks, factor,
    acts_ref, logits_ref, ids_ref, head_ref, gate_ref, up_ref, down_ref,
    grad_all, out_h, out_g, out_u, kept_out, mate_out,
    rows_in, w_gate, w_up, w_down, part, land1, land2, land3, delta,
    total, logit_buf, ids_buf, ids_turned, head_buf, logit_grad, turned, hidden_turned, staged,
    mate_send, mate_land, side_send, side_land,
    in_sem, own_sem, w_send, w_recv, x_send, x_recv, c_send, c_recv,
    s_send, s_recv, g_send, g_recv, o_local, o_send, o_recv, t_send, t_recv, xo_sem,
):
    row, col = lax.axis_index("row"), lax.axis_index("col")
    z, xh = row // 2, row % 2
    core, y, x = col % 2, (col // 2) % 4, col // 8
    g1, g2 = (y % 2 + y // 2) % 2, y // 2
    block = acts_ref.shape[0]
    half = chunks * WIDE
    feats = acts_ref.shape[1]
    mate = 1 - core
    col_x = col + 8 - 16 * x
    col_1 = x * 8 + (y + 1 - 2 * (y % 2)) * 2 + core
    col_2 = x * 8 + ((y + 3 + 2 * (y % 2)) % 4) * 2 + core
    up_z, dn_z = (z + 1) % 4, (z + 3) % 4
    peer_core = (row, col + 1 - 2 * core)
    peer_xh = (z * 2 + 1 - xh, col)
    peer_up = (up_z * 2 + xh, col)
    peer_dn = (dn_z * 2 + xh, col)

    barrier = pltpu.get_barrier_semaphore()
    for peer in (peer_core, peer_xh, peer_up, peer_dn, (row, col_x), (row, col_1), (row, col_2)):
        pl.semaphore_signal(barrier, inc=1, device_id=peer, device_id_type=MESH)

    def local(src, dst, sem):
        return pltpu.make_async_copy(src, dst, sem)

    def remote(src, dst, ssem, rsem, peer):
        return pltpu.make_async_remote_copy(
            src_ref=src, dst_ref=dst, send_sem=ssem, recv_sem=rsem, device_id=peer, device_id_type=MESH
        )

    def span(index):
        return pl.ds(pl.multiple_of(index * block, block), block)

    def held(name):
        return pl.ds(ORDER.index(name) * block, block)

    def side_of(index):
        return pl.ds(pl.multiple_of(index * feats, feats), feats)

    loads = (
        local(acts_ref, rows_in.at[0, held("own"), side_of(core)], in_sem.at[0]),
        local(logits_ref, logit_buf, in_sem.at[1]),
        local(ids_ref, ids_buf, in_sem.at[2]),
        local(head_ref, head_buf, in_sem.at[3]),
    )
    for load in loads:
        load.start()

    def chunk_of(ref, side, k, by_rows):
        at = pl.ds(pl.multiple_of(side * half + k * WIDE, WIDE), WIDE)
        return ref.at[at, :] if by_rows else ref.at[:, at]

    def weight_side(buf, k, by_rows):
        return buf.at[k, :, side_of(core)] if by_rows else buf.at[k, side_of(core), :]

    weights = ((gate_ref, w_gate, False), (up_ref, w_up, False), (down_ref, w_down, True))

    def own_weight(k, a):
        ref, buf, by_rows = weights[a]
        return local(chunk_of(ref, core, k, by_rows), weight_side(buf, k, by_rows), own_sem.at[k, a])

    def sent_weight(k, a):
        ref, buf, by_rows = weights[a]
        return remote(
            chunk_of(ref, mate, k, by_rows), weight_side(buf, k, by_rows), w_send.at[k, a], w_recv.at[k, a], peer_core
        )

    def start_weights(make):
        for arrays in ((0, 1), (2,)):
            def step(k, carry, arrays=arrays):
                for a in arrays:
                    make(k, a).start()
                return carry

            lax.fori_loop(0, chunks, step, 0)

    pl.semaphore_wait(barrier, 7)

    blocks = {
        "own": row, "mate": z * 2 + 1 - xh,
        "up": up_z * 2 + xh, "up_m": up_z * 2 + 1 - xh,
        "dn": dn_z * 2 + xh, "dn_m": dn_z * 2 + 1 - xh,
        "far": ((z + 2) % 4) * 2 + xh, "far_m": ((z + 2) % 4) * 2 + 1 - xh,
    }
    peers = {"xh": peer_xh, "up": peer_up, "dn": peer_dn}

    def gather_send(t, m):
        here, there, peer = MESSAGES[m]
        return remote(
            rows_in.at[t, held(here), side_of(core)], rows_in.at[t, held(there), side_of(core)],
            x_send.at[t, m], x_recv.at[t, m], peers[peer],
        )

    def to_core(t, m, side=core):
        ref = rows_in.at[t, held("own" if m == 7 else MESSAGES[m][1]), side_of(side)]
        return remote(ref, ref, c_send.at[t, m], c_recv.at[t, m], peer_core)

    def pass_on(t, m, *then):
        gather_send(t, m).wait_recv()
        for n in then:
            gather_send(t, n).start()
        to_core(t, m).start()

    def from_core(t, *ms):
        for m in ms:
            to_core(t, m, mate).wait_recv()

    loads[0].wait()
    for m in (0, 1, 2):
        gather_send(0, m).start()
    to_core(0, 7).start()
    start_weights(sent_weight)
    start_weights(own_weight)

    for load in loads[1:]:
        load.wait()
    ids_turned[...] = ids_buf[...].T
    codes = logit_buf.shape[1]
    step_rows = 16

    def logit_step(i, carry):
        at = pl.ds(pl.multiple_of(i * step_rows, step_rows), step_rows)
        ids = ids_turned[at, :]
        code = lax.broadcasted_iota(jnp.int32, (step_rows, codes), 1)
        hit = ids[:, 0:1] == code
        for label in range(1, ids.shape[1]):
            hit = jnp.logical_or(hit, ids[:, label : label + 1] == code)
        target = jnp.where(hit, 1.0, 0.0)
        logit_grad[at, :] = (jax.nn.sigmoid(logit_buf[at, :]) - target).astype(BF16)
        return carry

    lax.fori_loop(0, block // step_rows, logit_step, 0)
    rows_in[1, held("own"), side_of(core)] = jnp.dot(
        logit_grad[...], head_buf[...], preferred_element_type=F32
    ).astype(BF16)
    total[...] = jnp.zeros_like(total)
    gather_send(0, 2).wait_recv()
    gather_send(0, 6).start()
    for m in (0, 1, 2):
        gather_send(1, m).start()
    gather_send(0, 0).wait_recv()
    for m in (3, 4):
        gather_send(0, m).start()
    gather_send(0, 1).wait_recv()
    for m in (1, 2, 0):
        to_core(0, m).start()
    to_core(1, 7).start()

    def peer_of(dim):
        return (row, jnp.where(dim == 0, col_x, jnp.where(dim == 1, col_1, col_2)))

    def mod3(value):
        for step in (6, 3):
            value = jnp.where(value >= step, value - step, value)
        return value

    def turn(k, a):
        return mod3(k + a)

    def back_turn(k, a):
        return mod3(k + a + 2)

    bits = {
        name: ((b // 4 + x) % 2, (b // 2 + g1) % 2, (b + b // 2 + g2) % 2) for name, b in blocks.items()
    }

    def weights_of(r):
        return (
            jnp.where(r == 0, 4, jnp.where(r == 1, 1, 2)),
            jnp.where(r == 1, 4, jnp.where(r == 2, 1, 2)),
            jnp.where(r == 2, 4, jnp.where(r == 0, 1, 2)),
        )

    def slot_of(weights, name):
        return sum(w * bit for w, bit in zip(weights, bits[name]))

    def sum_send(step, k, a):
        size = (4, 2, 1)[step] * block
        dst = (land1, land2, land3)[step]
        return remote(
            part.at[k, a, pl.ds(size, size)], dst.at[k, a], s_send.at[step, k, a], s_recv.at[step, k, a],
            peer_of(mod3(turn(k, a) + step)),
        )

    def give_send(step, k, a):
        size = (4, 2, 1)[step] * block
        return remote(
            delta.at[k, a, pl.ds(0, size)], delta.at[k, a, pl.ds(size, size)], g_send.at[step, k, a], g_recv.at[step, k, a],
            peer_of(mod3(back_turn(k, a) + step)),
        )

    def got_weight(k, a):
        own_weight(k, a).wait()
        sent_weight(k, a).wait_recv()

    def forward_in(first, count, wait=False):
        def step(k, carry):
            for a, buf in ((0, w_gate), (1, w_up)):
                if wait:
                    got_weight(k, a)
                rows = rows_in[0, first * block : (first + count) * block, :]
                value = jnp.dot(rows, buf[k], preferred_element_type=F32).astype(BF16)
                places = weights_of(turn(k, a))
                for j in range(count):
                    slot = slot_of(places, ORDER[first + j])
                    part[k, a, span(slot), :] = value[j * block : (j + 1) * block]

                    @pl.when(slot >= 4)
                    def _():
                        remote(
                            part.at[k, a, span(slot)], land1.at[k, a, span(slot - 4)],
                            s_send.at[0, k, a], s_recv.at[0, k, a], peer_of(turn(k, a)),
                        ).start()

            return carry

        return step

    def forward_out(k):
        got_weight(k, 2)
        value = lax.dot_general(rows_in[1], w_down[k], NT, preferred_element_type=F32).astype(BF16)
        places = weights_of(turn(k, 2))
        for j, name in enumerate(ORDER):
            part[k, 2, span(slot_of(places, name)), :] = value[j * block : (j + 1) * block]
        sum_send(0, k, 2).start()

    from_core(0, 7, 1, 2)
    lax.fori_loop(0, chunks, forward_in(0, 3, True), 0)
    pass_on(0, 3, 5)
    pass_on(0, 6)
    pass_on(0, 4)
    pass_on(1, 2, 6)
    pass_on(1, 1)
    pass_on(1, 0, 3, 4)
    from_core(0, 0, 3, 4, 6)
    lax.fori_loop(0, chunks, forward_in(3, 4), 0)
    pass_on(0, 5)
    pass_on(1, 3, 5)
    pass_on(1, 6)
    pass_on(1, 4)
    from_core(0, 5)
    lax.fori_loop(0, chunks, forward_in(7, 1), 0)
    pass_on(1, 5)
    from_core(1, *range(8))
    def add_in(k, a, land, first, count):
        for b in range(first, first + count):
            at = pl.ds(b * block, block)
            part[k, a, at, :] = part[k, a, at, :] + land[k, a, at, :]

    def sum_stage(step, k, arrays=(0, 1, 2)):
        land = (land1, land2)[step]
        keep = (2, 1)[step]
        for a in arrays:
            sum_send(step, k, a).wait_recv()
            add_in(k, a, land, keep, keep)
            sum_send(step + 1, k, a).start()
            add_in(k, a, land, 0, keep)

    def activate(k):
        for a in range(3):
            sum_send(2, k, a).wait_recv()
        piece = 32

        def act_step(i, carry):
            at = pl.ds(pl.multiple_of(i * piece, piece), piece)
            gate, upper, back = (part[k, a, at, :].astype(F32) + land3[k, a, at, :].astype(F32) for a in range(3))
            sig = jax.nn.sigmoid(gate)
            silu = gate * sig
            delta[k, 0, at, :] = (back * upper * sig * (1.0 + gate * (1.0 - sig))).astype(BF16)
            delta[k, 1, at, :] = (back * silu).astype(BF16)
            delta[k, 2, at, :] = (silu * upper).astype(BF16)
            return carry

        lax.fori_loop(0, block // piece, act_step, 0)
        for a in range(3):
            give_send(2, k, a).start()

    def give_stage(step, k, arrays=(0, 1)):
        for a in arrays:
            give_send(step, k, a).wait_recv()
            give_send(step - 1, k, a).start()
            if a == 2:
                give_send(step, k, a).wait_send()

    outs = (out_g, out_u, out_h)

    def out_from(k, a, side):
        return hidden_turned.at[k] if a == 2 else staged.at[k % 2, a, side_of(side), :]

    def own_out(k, a):
        return local(out_from(k, a, core), chunk_of(outs[a], core, k, a == 2), o_local.at[k, a])

    def core_out(k, a, side=core):
        return remote(
            out_from(k, a, mate), chunk_of(outs[a], side, k, a == 2), o_send.at[k, a], o_recv.at[k, a], peer_core
        )

    def finish(k, a):
        give_send(0, k, a).wait_recv()
        for step in range(3):
            sum_send(step, k, a).wait_send()
        places = weights_of(back_turn(k, a))
        for name in ORDER:
            part[k, a, held(name), :] = delta[k, a, span(slot_of(places, name)), :]
        if a == 2:
            give_send(0, k, a).wait_send()
            tokens = 8 * block
            for at in range(0, tokens, 128):
                hidden_turned[k, :, at : at + 128] = part[k, 2, at : at + 128, :].T
            own_out(k, a).start()
            core_out(k, a).start()

    def backward(k):
        for a in range(2):
            finish(k, a)
        total[...] = (
            total[...]
            + lax.dot_general(part[k, 0], w_gate[k], NT, preferred_element_type=F32)
            + lax.dot_general(part[k, 1], w_up[k], NT, preferred_element_type=F32)
        )

    def gradients(k):
        for a in range(2):
            value = jnp.dot(turned[...], part[k, a], preferred_element_type=F32)
            staged[k % 2, a] = (value * factor).astype(BF16)
            own_out(k, a).start()
            core_out(k, a).start()

    def settle_out(k, a):
        own_out(k, a).wait()
        core_out(k, a).wait_send()
        core_out(k, a, mate).wait_recv()

    def settle(k):
        for a in range(2):
            for step in range(3):
                give_send(step, k, a).wait_send()
            settle_out(k, a)

    def settle_inputs():
        def step(k, carry):
            for a in range(3):
                sent_weight(k, a).wait_send()
            return carry

        lax.fori_loop(0, chunks, step, 0)
        for t in range(2):
            for m in range(7):
                gather_send(t, m).wait_send()
            for m in range(8):
                to_core(t, m).wait_send()
        grad_copy.wait()

    grad_copy = local(rows_in.at[1, :, side_of(core)], grad_all, xo_sem.at[0])

    def turn_inputs():
        grad_copy.start()
        for at in range(0, 2 * feats, 128):
            turned[at : at + 128, :] = rows_in[0, :, at : at + 128].T

    def late_give(first, last):
        def step(k, carry):
            give_stage(1, k, (2,))
            return carry

        lax.fori_loop(min(first, chunks), min(last, chunks), step, 0)

    ahead = min(3, chunks)

    def first_out(k, carry):
        forward_out(k)
        return carry

    def first_sums(k, carry):
        sum_stage(0, k, (0, 1))
        return carry

    lax.fori_loop(0, ahead, first_out, 0)
    lax.fori_loop(0, ahead, first_sums, 0)

    def slot_step(i, carry):
        @pl.when(i + ahead < chunks)
        def _():
            forward_out(i + ahead)
            sum_stage(0, i + ahead, (0, 1))

        def stage(lag, run):
            @pl.when(jnp.logical_and(i >= lag, i < chunks + lag))
            def _():
                run(i - lag)

        stage(0, lambda k: sum_stage(0, k, (2,)))
        stage(1, functools.partial(sum_stage, 1))
        stage(2, activate)
        stage(3, functools.partial(give_stage, 2))
        stage(4, functools.partial(give_stage, 1))
        stage(5, backward)
        stage(6, gradients)
        stage(7, settle)

        @pl.when(i == 2)
        def _():
            settle_inputs()

        @pl.when(i == 0)
        def _():
            turn_inputs()

        @pl.when(i >= chunks)
        def _():
            first = 2 * (i - chunks)
            for k in (first, first + 1):
                @pl.when(k < chunks)
                def _():
                    give_stage(2, k, (2,))

        @pl.when(i == chunks + 2)
        def _():
            late_give(0, 1)

        @pl.when(i == chunks + 3)
        def _():
            late_give(1, 4)

        return carry

    lax.fori_loop(0, chunks + 5, slot_step, 0)

    def late_finish(first, last):
        def step(k, carry):
            finish(k, 2)
            return carry

        lax.fori_loop(min(first, chunks), min(last, chunks), step, 0)

    late_give(4, chunks)

    cored = ("far", "far_m", "up_m", "dn", "up", "dn_m", "mate", "own")

    def core_sum(n):
        at = held(cored[n])
        return remote(mate_send.at[at], mate_land.at[at], t_send.at[7 + n], t_recv.at[7 + n], peer_core)

    for n, name in enumerate(cored):
        mate_send[held(name), :] = total[held(name), side_of(mate)].astype(BF16)
        core_sum(n).start()

    def core_add(n):
        core_sum(n).wait_recv()
        at = held(cored[n])
        both = total[at, side_of(core)] + mate_land[at, :].astype(F32)
        if n < 4:
            side_send[at, :] = both.astype(BF16)
        else:
            total[at, side_of(core)] = both

    def mine(name):
        return total[held(name), side_of(core)]

    def send_block(m, name, peer):
        return remote(side_send.at[held(name)], side_land.at[m], t_send.at[m], t_recv.at[m], peer)

    far_up = send_block(0, "far", peer_up)
    far_dn = send_block(1, "far_m", peer_dn)
    one_up = send_block(2, "up_m", peer_up)
    one_dn = send_block(3, "dn", peer_dn)
    two_up = send_block(4, "up", peer_up)
    two_dn = send_block(5, "dn_m", peer_dn)
    core_add(0)
    far_up.start()
    core_add(1)
    far_dn.start()
    core_add(2)
    one_up.start()
    core_add(3)
    one_dn.start()
    for n in range(4, 8):
        core_add(n)
    gradients(chunks - 1)
    late_finish(0, 2)
    far_up.wait_recv()
    side_send[held("up"), :] = (mine("up") + side_land[0].astype(F32)).astype(BF16)
    two_up.start()
    far_dn.wait_recv()
    side_send[held("dn_m"), :] = (mine("dn_m") + side_land[1].astype(F32)).astype(BF16)
    two_dn.start()
    late_finish(2, 4)
    one_up.wait_recv()
    two_dn.wait_recv()
    side_send[held("mate"), :] = (mine("mate") + side_land[2].astype(F32) + side_land[5].astype(F32)).astype(BF16)
    one_dn.wait_recv()
    two_up.wait_recv()
    total[held("own"), side_of(core)] = mine("own") + side_land[3].astype(F32) + side_land[4].astype(F32)
    results = (
        local(side_send.at[held("mate")], mate_out, xo_sem.at[2]),
        local(total.at[held("own"), side_of(core)], kept_out, xo_sem.at[3]),
    )
    for copy in results:
        copy.start()
    late_finish(4, chunks)

    for k in range(max(chunks - 2, 0), chunks):
        settle(k)

    def settle_hidden(k, carry):
        settle_out(k, 2)
        return carry

    lax.fori_loop(0, chunks, settle_hidden, 0)
    for n in range(8):
        core_sum(n).wait_send()
    for copy in (far_up, far_dn, one_up, one_dn, two_up, two_dn):
        copy.wait_send()
    for copy in results:
        copy.wait()


def grads_kernel(factor, gate_in, up_in, hidden, grad_all, gate_grad, up_grad, down_grad):
    gate_grad[...] = gate_in[...]
    up_grad[...] = up_in[...]
    down_grad[...] = (jnp.dot(hidden[...], grad_all[...], preferred_element_type=F32) * factor).astype(BF16)


def weight_grads(gate_grad, up_grad, hidden, grad_all):
    (feats, width), tokens = gate_grad.shape, grad_all.shape[0]
    steps = 4
    rows = pl.BlockSpec((feats // steps, width), lambda i: (i, 0))
    return pl.pallas_call(
        functools.partial(grads_kernel, 1.0 / tokens**0.5),
        grid=(steps,),
        out_shape=(
            jax.ShapeDtypeStruct((feats, width), BF16), jax.ShapeDtypeStruct((feats, width), BF16),
            jax.ShapeDtypeStruct((width, feats), BF16),
        ),
        in_specs=[
            rows, rows,
            pl.BlockSpec((width // steps, tokens), lambda i: (i, 0)),
            pl.BlockSpec((tokens, feats), lambda i: (0, 0)),
        ],
        out_specs=(rows, rows, pl.BlockSpec((width // steps, feats), lambda i: (i, 0))),
        compiler_params=pltpu.CompilerParams(vmem_limit_bytes=62 * 2**20),
        cost_estimate=pl.CostEstimate(
            flops=2 * tokens * feats * width, bytes_accessed=12 * feats * width, transcendentals=0
        ),
        name="grads_kernel",
    )(gate_grad, up_grad, hidden, grad_all)


def per_device(acts, logits, label_ids, head_weight, gate_weight, up_weight, down_weight):
    tokens = acts.shape[0] * 8
    width, feats = gate_weight.shape[1], acts.shape[1]
    block = acts.shape[0]
    chunks = width // 2 // WIDE
    any_spec = pl.BlockSpec(memory_space=pl.ANY)
    dma = pltpu.SemaphoreType.DMA
    grads_shape = jax.ShapeDtypeStruct((feats, width), BF16)
    rows_shape = jax.ShapeDtypeStruct((tokens, feats), BF16)
    grad_all, hidden, gate_grad, up_grad, kept, passed = pl.pallas_call(
        functools.partial(layer_kernel, chunks, 1.0 / tokens**0.5),
        out_shape=(
            rows_shape, jax.ShapeDtypeStruct((width, tokens), BF16), grads_shape, grads_shape,
            jax.ShapeDtypeStruct(acts.shape, F32), jax.ShapeDtypeStruct(acts.shape, BF16),
        ),
        in_specs=[any_spec] * 7,
        out_specs=(any_spec,) * 6,
        scratch_shapes=[
            pltpu.VMEM((2, tokens, 2 * feats), BF16),
            pltpu.VMEM((chunks, 2 * feats, WIDE), BF16),
            pltpu.VMEM((chunks, 2 * feats, WIDE), BF16),
            pltpu.VMEM((chunks, WIDE, 2 * feats), BF16),
            pltpu.VMEM((chunks, 3, tokens, WIDE), BF16),
            pltpu.VMEM((chunks, 3, 4 * block, WIDE), BF16),
            pltpu.VMEM((chunks, 3, 2 * block, WIDE), BF16),
            pltpu.VMEM((chunks, 3, block, WIDE), BF16),
            pltpu.VMEM((chunks, 3, tokens, WIDE), BF16),
            pltpu.VMEM((tokens, 2 * feats), F32),
            pltpu.VMEM(logits.shape, F32),
            pltpu.VMEM(label_ids.shape[::-1], jnp.int32),
            pltpu.VMEM(label_ids.shape, jnp.int32),
            pltpu.VMEM(head_weight.shape, BF16),
            pltpu.VMEM(logits.shape, BF16),
            pltpu.VMEM((2 * feats, tokens), BF16),
            pltpu.VMEM((chunks, WIDE, tokens), BF16),
            pltpu.VMEM((2, 2, 2 * feats, WIDE), BF16),
            pltpu.VMEM((tokens, feats), BF16),
            pltpu.VMEM((tokens, feats), BF16),
            pltpu.VMEM((tokens, feats), BF16),
            pltpu.VMEM((6, block, feats), BF16),
            dma((4,)), dma((chunks, 3)), dma((chunks, 3)), dma((chunks, 3)),
            dma((2, 7)), dma((2, 7)), dma((2, 8)), dma((2, 8)),
            dma((3, chunks, 3)), dma((3, chunks, 3)), dma((3, chunks, 3)), dma((3, chunks, 3)),
            dma((chunks, 3)), dma((chunks, 3)), dma((chunks, 3)), dma((15,)), dma((15,)), dma((4,)),
        ],
        compiler_params=pltpu.CompilerParams(collective_id=0, has_side_effects=True, vmem_limit_bytes=60 * 2**20),
        name="layer_kernel",
    )(acts, logits, label_ids.T, head_weight, gate_weight, up_weight, down_weight)
    swapped = lax.ppermute(passed, "row", [(at, at + 1 - 2 * (at % 2)) for at in range(8)])
    acts_grad = (kept + swapped.astype(F32)).astype(BF16)
    gate_grad, up_grad, down_grad = weight_grads(gate_grad, up_grad, hidden, grad_all)
    return acts_grad, gate_grad, up_grad, down_grad


def solution(mesh):
    placed = (
        P("row", "col"),
        P("row", None),
        P("row", None),
        P(None, "col"),
        P("col", "row"),
        P("col", "row"),
        P("row", "col"),
    )
    return jax.shard_map(
        per_device,
        mesh=mesh,
        in_specs=placed,
        out_specs=(P("row", "col"), P("col", "row"), P("col", "row"), P("row", "col")),
        check_vma=False,
    )
```

```python
import functools

import jax
import jax.numpy as jnp
from jax import lax
from jax.experimental import pallas as pl
from jax.experimental.pallas import tpu as pltpu
from jax.sharding import PartitionSpec as P

MESH = pl.DeviceIdType.MESH
BF16 = jnp.bfloat16
F32 = jnp.float32
WIDE = 256
NT = (((1,), (1,)), ((), ()))
ORDER = ("own", "up", "dn", "mate", "far", "up_m", "dn_m", "far_m")
MESSAGES = (
    ("own", "mate", "xh"),
    ("own", "dn", "up"),
    ("own", "up", "dn"),
    ("mate", "dn_m", "up"),
    ("mate", "up_m", "dn"),
    ("dn_m", "far_m", "up"),
    ("up", "far", "dn"),
)


def layer_kernel(
    chunks, factor,
    acts_ref, logits_ref, ids_ref, head_ref, gate_ref, up_ref, down_ref,
    out_h, out_g, out_u, kept_out, mate_out,
    rows_in, w_gate, w_up, w_down, part, land1, land2, land3, delta,
    total, logit_buf, ids_buf, ids_turned, head_buf, logit_grad, turned, hidden_turned, staged, staged_down,
    mate_send, mate_land, side_send, side_land,
    in_sem, own_sem, w_send, w_recv, x_send, x_recv, c_send, c_recv,
    s_send, s_recv, g_send, g_recv, o_local, o_send, o_recv, t_send, t_recv, xo_sem,
):
    row, col = lax.axis_index("row"), lax.axis_index("col")
    z, xh = row // 2, row % 2
    core, y, x = col % 2, (col // 2) % 4, col // 8
    g1, g2 = (y % 2 + y // 2) % 2, y // 2
    block = acts_ref.shape[0]
    half = chunks * WIDE
    feats = acts_ref.shape[1]
    mate = 1 - core
    col_x = col + 8 - 16 * x
    col_1 = x * 8 + (y + 1 - 2 * (y % 2)) * 2 + core
    col_2 = x * 8 + ((y + 3 + 2 * (y % 2)) % 4) * 2 + core
    up_z, dn_z = (z + 1) % 4, (z + 3) % 4
    peer_core = (row, col + 1 - 2 * core)
    peer_xh = (z * 2 + 1 - xh, col)
    peer_up = (up_z * 2 + xh, col)
    peer_dn = (dn_z * 2 + xh, col)

    barrier = pltpu.get_barrier_semaphore()
    for peer in (peer_core, peer_xh, peer_up, peer_dn, (row, col_x), (row, col_1), (row, col_2)):
        pl.semaphore_signal(barrier, inc=1, device_id=peer, device_id_type=MESH)

    def local(src, dst, sem):
        return pltpu.make_async_copy(src, dst, sem)

    def remote(src, dst, ssem, rsem, peer):
        return pltpu.make_async_remote_copy(
            src_ref=src, dst_ref=dst, send_sem=ssem, recv_sem=rsem, device_id=peer, device_id_type=MESH
        )

    def span(index):
        return pl.ds(pl.multiple_of(index * block, block), block)

    def held(name):
        return pl.ds(ORDER.index(name) * block, block)

    def side_of(index):
        return pl.ds(pl.multiple_of(index * feats, feats), feats)

    loads = (
        local(acts_ref, rows_in.at[0, held("own"), side_of(core)], in_sem.at[0]),
        local(logits_ref, logit_buf, in_sem.at[1]),
        local(ids_ref, ids_buf, in_sem.at[2]),
        local(head_ref, head_buf, in_sem.at[3]),
    )
    for load in loads:
        load.start()

    def chunk_of(ref, side, k, by_rows):
        at = pl.ds(pl.multiple_of(side * half + k * WIDE, WIDE), WIDE)
        return ref.at[at, :] if by_rows else ref.at[:, at]

    def weight_side(buf, k, by_rows):
        return buf.at[k, :, side_of(core)] if by_rows else buf.at[k, side_of(core), :]

    weights = ((gate_ref, w_gate, False), (up_ref, w_up, False), (down_ref, w_down, True))

    def own_weight(k, a):
        ref, buf, by_rows = weights[a]
        return local(chunk_of(ref, core, k, by_rows), weight_side(buf, k, by_rows), own_sem.at[k, a])

    def sent_weight(k, a):
        ref, buf, by_rows = weights[a]
        return remote(
            chunk_of(ref, mate, k, by_rows), weight_side(buf, k, by_rows), w_send.at[k, a], w_recv.at[k, a], peer_core
        )

    def start_weights(make, arrays, first, last):
        def step(k, carry):
            for a in arrays:
                make(k, a).start()
            return carry

        lax.fori_loop(min(first, chunks), min(last, chunks), step, 0)

    pl.semaphore_wait(barrier, 7)

    blocks = {
        "own": row, "mate": z * 2 + 1 - xh,
        "up": up_z * 2 + xh, "up_m": up_z * 2 + 1 - xh,
        "dn": dn_z * 2 + xh, "dn_m": dn_z * 2 + 1 - xh,
        "far": ((z + 2) % 4) * 2 + xh, "far_m": ((z + 2) % 4) * 2 + 1 - xh,
    }
    peers = {"xh": peer_xh, "up": peer_up, "dn": peer_dn}

    def gather_send(t, m):
        here, there, peer = MESSAGES[m]
        return remote(
            rows_in.at[t, held(here), side_of(core)], rows_in.at[t, held(there), side_of(core)],
            x_send.at[t, m], x_recv.at[t, m], peers[peer],
        )

    def to_core(t, m, side=core):
        ref = rows_in.at[t, held("own" if m == 7 else MESSAGES[m][1]), side_of(side)]
        return remote(ref, ref, c_send.at[t, m], c_recv.at[t, m], peer_core)

    def pass_on(t, m, *then):
        gather_send(t, m).wait_recv()
        for n in then:
            gather_send(t, n).start()
        to_core(t, m).start()

    def from_core(t, *ms):
        for m in ms:
            to_core(t, m, mate).wait_recv()

    loads[0].wait()
    for m in (0, 1, 2):
        gather_send(0, m).start()
    to_core(0, 7).start()
    start_weights(sent_weight, (0, 1), 0, chunks)
    start_weights(own_weight, (0, 1), 0, chunks)

    for load in loads[1:]:
        load.wait()
    ids_turned[...] = ids_buf[...].T
    codes = logit_buf.shape[1]
    step_rows = 16

    def logit_step(i, carry):
        at = pl.ds(pl.multiple_of(i * step_rows, step_rows), step_rows)
        ids = ids_turned[at, :]
        code = lax.broadcasted_iota(jnp.int32, (step_rows, codes), 1)
        hit = ids[:, 0:1] == code
        for label in range(1, ids.shape[1]):
            hit = jnp.logical_or(hit, ids[:, label : label + 1] == code)
        target = jnp.where(hit, 1.0, 0.0)
        logit_grad[at, :] = (jax.nn.sigmoid(logit_buf[at, :]) - target).astype(BF16)
        return carry

    lax.fori_loop(0, block // step_rows, logit_step, 0)
    gather_send(0, 2).wait_recv()
    gather_send(0, 6).start()
    to_core(0, 2).start()
    rows_in[1, held("own"), side_of(core)] = jnp.dot(
        logit_grad[...], head_buf[...], preferred_element_type=F32
    ).astype(BF16)
    for m in (0, 1, 2):
        gather_send(1, m).start()
    gather_send(0, 1).wait_recv()
    to_core(0, 1).start()
    to_core(1, 7).start()
    total[...] = jnp.zeros_like(total)

    def peer_of(dim):
        return (row, jnp.where(dim == 0, col_x, jnp.where(dim == 1, col_1, col_2)))

    def mod3(value):
        for step in (6, 3):
            value = jnp.where(value >= step, value - step, value)
        return value

    def turn(k, a):
        return mod3(k + a)

    def back_turn(k, a):
        return mod3(k + a + 2)

    bits = {
        name: ((b // 4 + x) % 2, (b // 2 + g1) % 2, (b + b // 2 + g2) % 2) for name, b in blocks.items()
    }

    def weights_of(r):
        return (
            jnp.where(r == 0, 4, jnp.where(r == 1, 1, 2)),
            jnp.where(r == 1, 4, jnp.where(r == 2, 1, 2)),
            jnp.where(r == 2, 4, jnp.where(r == 0, 1, 2)),
        )

    def slot_of(weights, name):
        return sum(w * bit for w, bit in zip(weights, bits[name]))

    def sum_send(step, k, a):
        size = (4, 2, 1)[step] * block
        dst = (land1, land2, land3)[step]
        return remote(
            part.at[k, a, pl.ds(size, size)], dst.at[k, a], s_send.at[step, k, a], s_recv.at[step, k, a],
            peer_of(mod3(turn(k, a) + step)),
        )

    def give_send(step, k, a):
        size = (4, 2, 1)[step] * block
        return remote(
            delta.at[k, a, pl.ds(0, size)], delta.at[k, a, pl.ds(size, size)], g_send.at[step, k, a], g_recv.at[step, k, a],
            peer_of(mod3(back_turn(k, a) + step)),
        )

    def got_weight(k, a):
        own_weight(k, a).wait()
        sent_weight(k, a).wait_recv()

    def forward_in(first, count, wait=False):
        def step(k, carry):
            for a, buf in ((0, w_gate), (1, w_up)):
                if wait:
                    got_weight(k, a)
                rows = rows_in[0, first * block : (first + count) * block, :]
                value = jnp.dot(rows, buf[k], preferred_element_type=F32).astype(BF16)
                places = weights_of(turn(k, a))
                for j in range(count):
                    slot = slot_of(places, ORDER[first + j])
                    part[k, a, span(slot), :] = value[j * block : (j + 1) * block]

                    @pl.when(slot >= 4)
                    def _():
                        remote(
                            part.at[k, a, span(slot)], land1.at[k, a, span(slot - 4)],
                            s_send.at[0, k, a], s_recv.at[0, k, a], peer_of(turn(k, a)),
                        ).start()

            return carry

        return step

    def forward_out(k):
        got_weight(k, 2)
        value = lax.dot_general(rows_in[1], w_down[k], NT, preferred_element_type=F32).astype(BF16)
        places = weights_of(turn(k, 2))
        for j, name in enumerate(ORDER):
            part[k, 2, span(slot_of(places, name)), :] = value[j * block : (j + 1) * block]
        sum_send(0, k, 2).start()

    pass_on(0, 0, 3, 4)
    from_core(0, 7, 1, 2)
    lax.fori_loop(0, chunks, forward_in(0, 3, True), 0)
    pass_on(0, 3, 5)
    pass_on(0, 6)
    pass_on(0, 4)
    pass_on(1, 2, 6)
    pass_on(1, 1)
    pass_on(1, 0, 3, 4)
    start_weights(own_weight, (2,), 0, chunks)
    start_weights(sent_weight, (2,), 0, chunks)
    from_core(0, 0, 3, 4, 6)
    lax.fori_loop(0, chunks, forward_in(3, 4), 0)
    pass_on(0, 5)
    pass_on(1, 3, 5)
    pass_on(1, 6)
    pass_on(1, 4)
    from_core(0, 5)
    lax.fori_loop(0, chunks, forward_in(7, 1), 0)
    pass_on(1, 5)
    from_core(1, *range(8))
    def add_in(k, a, land, first, count):
        for b in range(first, first + count):
            at = pl.ds(b * block, block)
            part[k, a, at, :] = part[k, a, at, :] + land[k, a, at, :]

    def sum_stage(step, k, arrays=(0, 1, 2)):
        land = (land1, land2)[step]
        keep = (2, 1)[step]
        for a in arrays:
            sum_send(step, k, a).wait_recv()
            add_in(k, a, land, keep, keep)
            sum_send(step + 1, k, a).start()
            add_in(k, a, land, 0, keep)

    def activate(k):
        for a in range(3):
            sum_send(2, k, a).wait_recv()
        piece = 32

        def act_step(i, carry):
            at = pl.ds(pl.multiple_of(i * piece, piece), piece)
            gate, upper, back = (part[k, a, at, :].astype(F32) + land3[k, a, at, :].astype(F32) for a in range(3))
            sig = jax.nn.sigmoid(gate)
            silu = gate * sig
            delta[k, 0, at, :] = (back * upper * sig * (1.0 + gate * (1.0 - sig))).astype(BF16)
            delta[k, 1, at, :] = (back * silu).astype(BF16)
            delta[k, 2, at, :] = (silu * upper).astype(BF16)
            return carry

        lax.fori_loop(0, block // piece, act_step, 0)
        for a in range(3):
            give_send(2, k, a).start()

    def give_stage(step, k, arrays=(0, 1)):
        for a in arrays:
            give_send(step, k, a).wait_recv()
            give_send(step - 1, k, a).start()
            if a == 2:
                give_send(step, k, a).wait_send()

    outs = (out_g, out_u, out_h)

    def out_from(k, a, side):
        return staged_down.at[k, :, side_of(side)] if a == 2 else staged.at[k % 2, a, side_of(side), :]

    def own_out(k, a):
        return local(out_from(k, a, core), chunk_of(outs[a], core, k, a == 2), o_local.at[k, a])

    def core_out(k, a, side=core):
        return remote(
            out_from(k, a, mate), chunk_of(outs[a], side, k, a == 2), o_send.at[k, a], o_recv.at[k, a], peer_core
        )

    def finish(k, a):
        give_send(0, k, a).wait_recv()
        for step in range(3):
            sum_send(step, k, a).wait_send()
        places = weights_of(back_turn(k, a))
        for name in ORDER:
            part[k, a, held(name), :] = delta[k, a, span(slot_of(places, name)), :]
        if a == 2:
            give_send(0, k, a).wait_send()
            tokens = 8 * block
            for at in range(0, tokens, 128):
                hidden_turned[:, at : at + 128] = part[k, 2, at : at + 128, :].T
            value = jnp.dot(hidden_turned[...], rows_in[1], preferred_element_type=F32)
            staged_down[k] = (value * factor).astype(BF16)
            own_out(k, a).start()
            core_out(k, a).start()

    def backward(k):
        for a in range(2):
            finish(k, a)
        total[...] = (
            total[...]
            + lax.dot_general(part[k, 0], w_gate[k], NT, preferred_element_type=F32)
            + lax.dot_general(part[k, 1], w_up[k], NT, preferred_element_type=F32)
        )

    def gradients(k):
        for a in range(2):
            value = jnp.dot(turned[...], part[k, a], preferred_element_type=F32)
            staged[k % 2, a] = (value * factor).astype(BF16)
            own_out(k, a).start()
            core_out(k, a).start()

    def settle_out(k, a):
        own_out(k, a).wait()
        core_out(k, a).wait_send()
        core_out(k, a, mate).wait_recv()

    def settle(k):
        for a in range(2):
            for step in range(3):
                give_send(step, k, a).wait_send()
            settle_out(k, a)

    def settle_inputs():
        def step(k, carry):
            for a in range(3):
                sent_weight(k, a).wait_send()
            return carry

        lax.fori_loop(0, chunks, step, 0)
        for t in range(2):
            for m in range(7):
                gather_send(t, m).wait_send()
            for m in range(8):
                to_core(t, m).wait_send()

    def turn_inputs():
        for at in range(0, 2 * feats, 128):
            turned[at : at + 128, :] = rows_in[0, :, at : at + 128].T

    def late_give(first, last):
        def step(k, carry):
            give_stage(1, k, (2,))
            return carry

        lax.fori_loop(min(first, chunks), min(last, chunks), step, 0)

    ahead = min(3, chunks)

    def first_out(k, carry):
        forward_out(k)
        return carry

    def first_sums(k, carry):
        sum_stage(0, k, (0, 1))
        return carry

    lax.fori_loop(0, ahead, first_out, 0)
    lax.fori_loop(0, ahead, first_sums, 0)

    def slot_step(i, carry):
        @pl.when(i + ahead < chunks)
        def _():
            forward_out(i + ahead)
            sum_stage(0, i + ahead, (0, 1))

        def stage(lag, run):
            @pl.when(jnp.logical_and(i >= lag, i < chunks + lag))
            def _():
                run(i - lag)

        stage(0, lambda k: sum_stage(0, k, (2,)))
        stage(1, functools.partial(sum_stage, 1))
        stage(2, activate)
        stage(3, functools.partial(give_stage, 2))
        stage(4, functools.partial(give_stage, 1))
        stage(5, backward)
        stage(6, gradients)
        stage(7, settle)

        @pl.when(i == 2)
        def _():
            settle_inputs()

        @pl.when(i == 0)
        def _():
            turn_inputs()

        @pl.when(i >= chunks)
        def _():
            first = 2 * (i - chunks)
            for k in (first, first + 1):
                @pl.when(k < chunks)
                def _():
                    give_stage(2, k, (2,))

        @pl.when(i == chunks + 3)
        def _():
            late_give(0, 3)

        return carry

    lax.fori_loop(0, chunks + 5, slot_step, 0)

    def late_finish(first, last):
        def step(k, carry):
            finish(k, 2)
            return carry

        lax.fori_loop(min(first, chunks), min(last, chunks), step, 0)

    late_give(3, chunks)

    cored = ("far", "far_m", "up_m", "dn", "up", "dn_m", "mate", "own")

    def core_sum(n):
        at = held(cored[n])
        return remote(mate_send.at[at], mate_land.at[at], t_send.at[7 + n], t_recv.at[7 + n], peer_core)

    for n, name in enumerate(cored):
        mate_send[held(name), :] = total[held(name), side_of(mate)].astype(BF16)
        core_sum(n).start()

    def core_add(n):
        core_sum(n).wait_recv()
        at = held(cored[n])
        both = total[at, side_of(core)] + mate_land[at, :].astype(F32)
        if n < 4:
            side_send[at, :] = both.astype(BF16)
        else:
            total[at, side_of(core)] = both

    def mine(name):
        return total[held(name), side_of(core)]

    def send_block(m, name, peer):
        return remote(side_send.at[held(name)], side_land.at[m], t_send.at[m], t_recv.at[m], peer)

    far_up = send_block(0, "far", peer_up)
    far_dn = send_block(1, "far_m", peer_dn)
    one_up = send_block(2, "up_m", peer_up)
    one_dn = send_block(3, "dn", peer_dn)
    two_up = send_block(4, "up", peer_up)
    two_dn = send_block(5, "dn_m", peer_dn)
    core_add(0)
    far_up.start()
    core_add(1)
    far_dn.start()
    core_add(2)
    one_up.start()
    core_add(3)
    one_dn.start()
    for n in range(4, 8):
        core_add(n)
    gradients(chunks - 1)
    late_finish(0, 2)
    far_up.wait_recv()
    side_send[held("up"), :] = (mine("up") + side_land[0].astype(F32)).astype(BF16)
    two_up.start()
    far_dn.wait_recv()
    side_send[held("dn_m"), :] = (mine("dn_m") + side_land[1].astype(F32)).astype(BF16)
    two_dn.start()
    late_finish(2, 6)
    one_up.wait_recv()
    two_dn.wait_recv()
    side_send[held("mate"), :] = (mine("mate") + side_land[2].astype(F32) + side_land[5].astype(F32)).astype(BF16)
    one_dn.wait_recv()
    two_up.wait_recv()
    total[held("own"), side_of(core)] = mine("own") + side_land[3].astype(F32) + side_land[4].astype(F32)
    results = (
        local(side_send.at[held("mate")], mate_out, xo_sem.at[0]),
        local(total.at[held("own"), side_of(core)], kept_out, xo_sem.at[1]),
    )
    for copy in results:
        copy.start()
    late_finish(6, chunks)

    for k in range(max(chunks - 2, 0), chunks):
        settle(k)

    def settle_hidden(k, carry):
        settle_out(k, 2)
        return carry

    lax.fori_loop(0, chunks, settle_hidden, 0)
    for n in range(8):
        core_sum(n).wait_send()
    for copy in (far_up, far_dn, one_up, one_dn, two_up, two_dn):
        copy.wait_send()
    for copy in results:
        copy.wait()


def pass_kernel(gate_in, up_in, down_in, gate_grad, up_grad, down_grad):
    gate_grad[...] = gate_in[...]
    up_grad[...] = up_in[...]
    down_grad[...] = down_in[...]


def pass_through(*grads):
    steps = 4
    rows = [pl.BlockSpec((grad.shape[0] // steps, grad.shape[1]), lambda i: (i, 0)) for grad in grads]
    return pl.pallas_call(
        pass_kernel,
        grid=(steps,),
        out_shape=[jax.ShapeDtypeStruct(grad.shape, BF16) for grad in grads],
        in_specs=rows,
        out_specs=rows,
        compiler_params=pltpu.CompilerParams(vmem_limit_bytes=62 * 2**20),
        cost_estimate=pl.CostEstimate(
            flops=0, bytes_accessed=4 * sum(grad.size for grad in grads), transcendentals=0
        ),
        name="pass_kernel",
    )(*grads)


def per_device(acts, logits, label_ids, head_weight, gate_weight, up_weight, down_weight):
    tokens = acts.shape[0] * 8
    width, feats = gate_weight.shape[1], acts.shape[1]
    block = acts.shape[0]
    chunks = width // 2 // WIDE
    any_spec = pl.BlockSpec(memory_space=pl.ANY)
    dma = pltpu.SemaphoreType.DMA
    grads_shape = jax.ShapeDtypeStruct((feats, width), BF16)
    down_grad, gate_grad, up_grad, kept, passed = pl.pallas_call(
        functools.partial(layer_kernel, chunks, 1.0 / tokens**0.5),
        out_shape=(
            jax.ShapeDtypeStruct((width, feats), BF16), grads_shape, grads_shape,
            jax.ShapeDtypeStruct(acts.shape, F32), jax.ShapeDtypeStruct(acts.shape, BF16),
        ),
        in_specs=[any_spec] * 7,
        out_specs=(any_spec,) * 5,
        scratch_shapes=[
            pltpu.VMEM((2, tokens, 2 * feats), BF16),
            pltpu.VMEM((chunks, 2 * feats, WIDE), BF16),
            pltpu.VMEM((chunks, 2 * feats, WIDE), BF16),
            pltpu.VMEM((chunks, WIDE, 2 * feats), BF16),
            pltpu.VMEM((chunks, 3, tokens, WIDE), BF16),
            pltpu.VMEM((chunks, 3, 4 * block, WIDE), BF16),
            pltpu.VMEM((chunks, 3, 2 * block, WIDE), BF16),
            pltpu.VMEM((chunks, 3, block, WIDE), BF16),
            pltpu.VMEM((chunks, 3, tokens, WIDE), BF16),
            pltpu.VMEM((tokens, 2 * feats), F32),
            pltpu.VMEM(logits.shape, F32),
            pltpu.VMEM(label_ids.shape[::-1], jnp.int32),
            pltpu.VMEM(label_ids.shape, jnp.int32),
            pltpu.VMEM(head_weight.shape, BF16),
            pltpu.VMEM(logits.shape, BF16),
            pltpu.VMEM((2 * feats, tokens), BF16),
            pltpu.VMEM((WIDE, tokens), BF16),
            pltpu.VMEM((2, 2, 2 * feats, WIDE), BF16),
            pltpu.VMEM((chunks, WIDE, 2 * feats), BF16),
            pltpu.VMEM((tokens, feats), BF16),
            pltpu.VMEM((tokens, feats), BF16),
            pltpu.VMEM((tokens, feats), BF16),
            pltpu.VMEM((6, block, feats), BF16),
            dma((4,)), dma((chunks, 3)), dma((chunks, 3)), dma((chunks, 3)),
            dma((2, 7)), dma((2, 7)), dma((2, 8)), dma((2, 8)),
            dma((3, chunks, 3)), dma((3, chunks, 3)), dma((3, chunks, 3)), dma((3, chunks, 3)),
            dma((chunks, 3)), dma((chunks, 3)), dma((chunks, 3)), dma((15,)), dma((15,)), dma((2,)),
        ],
        compiler_params=pltpu.CompilerParams(collective_id=0, has_side_effects=True, vmem_limit_bytes=60 * 2**20),
        name="layer_kernel",
    )(acts, logits, label_ids.T, head_weight, gate_weight, up_weight, down_weight)
    swapped = lax.ppermute(passed, "row", [(at, at + 1 - 2 * (at % 2)) for at in range(8)])
    acts_grad = (kept + swapped.astype(F32)).astype(BF16)
    gate_grad, up_grad, down_grad = pass_through(gate_grad, up_grad, down_grad)
    return acts_grad, gate_grad, up_grad, down_grad


def solution(mesh):
    placed = (
        P("row", "col"),
        P("row", None),
        P("row", None),
        P(None, "col"),
        P("col", "row"),
        P("col", "row"),
        P("row", "col"),
    )
    return jax.shard_map(
        per_device,
        mesh=mesh,
        in_specs=placed,
        out_specs=(P("row", "col"), P("col", "row"), P("col", "row"), P("row", "col")),
        check_vma=False,
    )
```

```python
import functools

import jax
import jax.numpy as jnp
from jax import lax
from jax.experimental import pallas as pl
from jax.experimental.pallas import tpu as pltpu
from jax.sharding import PartitionSpec as P

MESH = pl.DeviceIdType.MESH
BF16 = jnp.bfloat16
F32 = jnp.float32
WIDE = 256
NT = (((1,), (1,)), ((), ()))
ORDER = ("own", "up", "dn", "mate", "far", "up_m", "dn_m", "far_m")
MESSAGES = (
    ("own", "mate", "xh"),
    ("own", "dn", "up"),
    ("own", "up", "dn"),
    ("mate", "dn_m", "up"),
    ("mate", "up_m", "dn"),
    ("dn_m", "far_m", "up"),
    ("up", "far", "dn"),
)


def layer_kernel(
    chunks, factor,
    acts_ref, logits_ref, ids_ref, head_ref, gate_ref, up_ref, down_ref,
    out_h, out_g, out_u, kept_out, mate_out,
    rows_in, w_gate, w_up, w_down, part, land1, land2, land3, delta,
    total, logit_buf, ids_buf, ids_turned, head_buf, logit_grad, turned, hidden_turned, staged, staged_down,
    mate_send, mate_land, side_send, side_land,
    in_sem, own_sem, w_send, w_recv, x_send, x_recv, c_send, c_recv,
    s_send, s_recv, g_send, g_recv, o_local, o_send, o_recv, t_send, t_recv, xo_sem,
):
    row, col = lax.axis_index("row"), lax.axis_index("col")
    z, xh = row // 2, row % 2
    core, y, x = col % 2, (col // 2) % 4, col // 8
    g1, g2 = (y % 2 + y // 2) % 2, y // 2
    block = acts_ref.shape[0]
    half = chunks * WIDE
    feats = acts_ref.shape[1]
    mate = 1 - core
    col_x = col + 8 - 16 * x
    col_1 = x * 8 + (y + 1 - 2 * (y % 2)) * 2 + core
    col_2 = x * 8 + ((y + 3 + 2 * (y % 2)) % 4) * 2 + core
    up_z, dn_z = (z + 1) % 4, (z + 3) % 4
    peer_core = (row, col + 1 - 2 * core)
    peer_xh = (z * 2 + 1 - xh, col)
    peer_up = (up_z * 2 + xh, col)
    peer_dn = (dn_z * 2 + xh, col)

    barrier = pltpu.get_barrier_semaphore()
    for peer in (peer_core, peer_xh, peer_up, peer_dn, (row, col_x), (row, col_1), (row, col_2)):
        pl.semaphore_signal(barrier, inc=1, device_id=peer, device_id_type=MESH)

    def local(src, dst, sem):
        return pltpu.make_async_copy(src, dst, sem)

    def remote(src, dst, ssem, rsem, peer):
        return pltpu.make_async_remote_copy(
            src_ref=src, dst_ref=dst, send_sem=ssem, recv_sem=rsem, device_id=peer, device_id_type=MESH
        )

    def span(index):
        return pl.ds(pl.multiple_of(index * block, block), block)

    def held(name):
        return pl.ds(ORDER.index(name) * block, block)

    def side_of(index):
        return pl.ds(pl.multiple_of(index * feats, feats), feats)

    loads = (
        local(acts_ref, rows_in.at[0, held("own"), side_of(core)], in_sem.at[0]),
        local(logits_ref, logit_buf, in_sem.at[1]),
        local(ids_ref, ids_buf, in_sem.at[2]),
        local(head_ref, head_buf, in_sem.at[3]),
    )
    for load in loads:
        load.start()

    def chunk_of(ref, side, k, by_rows):
        at = pl.ds(pl.multiple_of(side * half + k * WIDE, WIDE), WIDE)
        return ref.at[at, :] if by_rows else ref.at[:, at]

    def weight_side(buf, k, by_rows):
        return buf.at[k, :, side_of(core)] if by_rows else buf.at[k, side_of(core), :]

    weights = ((gate_ref, w_gate, False), (up_ref, w_up, False), (down_ref, w_down, True))

    def own_weight(k, a):
        ref, buf, by_rows = weights[a]
        return local(chunk_of(ref, core, k, by_rows), weight_side(buf, k, by_rows), own_sem.at[k, a])

    def sent_weight(k, a):
        ref, buf, by_rows = weights[a]
        return remote(
            chunk_of(ref, mate, k, by_rows), weight_side(buf, k, by_rows), w_send.at[k, a], w_recv.at[k, a], peer_core
        )

    def start_weights(make, arrays, first, last):
        def step(k, carry):
            for a in arrays:
                make(k, a).start()
            return carry

        lax.fori_loop(min(first, chunks), min(last, chunks), step, 0)

    pl.semaphore_wait(barrier, 7)

    blocks = {
        "own": row, "mate": z * 2 + 1 - xh,
        "up": up_z * 2 + xh, "up_m": up_z * 2 + 1 - xh,
        "dn": dn_z * 2 + xh, "dn_m": dn_z * 2 + 1 - xh,
        "far": ((z + 2) % 4) * 2 + xh, "far_m": ((z + 2) % 4) * 2 + 1 - xh,
    }
    peers = {"xh": peer_xh, "up": peer_up, "dn": peer_dn}

    def gather_send(t, m):
        here, there, peer = MESSAGES[m]
        return remote(
            rows_in.at[t, held(here), side_of(core)], rows_in.at[t, held(there), side_of(core)],
            x_send.at[t, m], x_recv.at[t, m], peers[peer],
        )

    def to_core(t, m, side=core):
        ref = rows_in.at[t, held("own" if m == 7 else MESSAGES[m][1]), side_of(side)]
        return remote(ref, ref, c_send.at[t, m], c_recv.at[t, m], peer_core)

    def pass_on(t, m, *then):
        gather_send(t, m).wait_recv()
        for n in then:
            gather_send(t, n).start()
        to_core(t, m).start()

    def from_core(t, *ms):
        for m in ms:
            to_core(t, m, mate).wait_recv()

    loads[0].wait()
    for m in (0, 1, 2):
        gather_send(0, m).start()
    to_core(0, 7).start()
    start_weights(sent_weight, (0, 1), 0, chunks)
    start_weights(own_weight, (0, 1), 0, chunks)

    for load in loads[1:]:
        load.wait()
    ids_turned[...] = ids_buf[...].T
    codes = logit_buf.shape[1]
    step_rows = 16

    def logit_step(i, carry):
        at = pl.ds(pl.multiple_of(i * step_rows, step_rows), step_rows)
        ids = ids_turned[at, :]
        code = lax.broadcasted_iota(jnp.int32, (step_rows, codes), 1)
        hit = ids[:, 0:1] == code
        for label in range(1, ids.shape[1]):
            hit = jnp.logical_or(hit, ids[:, label : label + 1] == code)
        target = jnp.where(hit, 1.0, 0.0)
        logit_grad[at, :] = (jax.nn.sigmoid(logit_buf[at, :]) - target).astype(BF16)
        return carry

    lax.fori_loop(0, block // step_rows, logit_step, 0)
    gather_send(0, 2).wait_recv()
    gather_send(0, 6).start()
    to_core(0, 2).start()
    rows_in[1, held("own"), side_of(core)] = jnp.dot(
        logit_grad[...], head_buf[...], preferred_element_type=F32
    ).astype(BF16)
    for m in (0, 1, 2):
        gather_send(1, m).start()
    gather_send(0, 1).wait_recv()
    to_core(0, 1).start()
    to_core(1, 7).start()
    total[...] = jnp.zeros_like(total)

    def peer_of(dim):
        return (row, jnp.where(dim == 0, col_x, jnp.where(dim == 1, col_1, col_2)))

    def mod3(value):
        for step in (6, 3):
            value = jnp.where(value >= step, value - step, value)
        return value

    def turn(k, a):
        return mod3(k + a)

    def back_turn(k, a):
        return mod3(k + a + 2)

    bits = {
        name: ((b // 4 + x) % 2, (b // 2 + g1) % 2, (b + b // 2 + g2) % 2) for name, b in blocks.items()
    }

    def weights_of(r):
        return (
            jnp.where(r == 0, 4, jnp.where(r == 1, 1, 2)),
            jnp.where(r == 1, 4, jnp.where(r == 2, 1, 2)),
            jnp.where(r == 2, 4, jnp.where(r == 0, 1, 2)),
        )

    def slot_of(weights, name):
        return sum(w * bit for w, bit in zip(weights, bits[name]))

    def sum_send(step, k, a):
        size = (4, 2, 1)[step] * block
        dst = (land1, land2, land3)[step]
        return remote(
            part.at[k, a, pl.ds(size, size)], dst.at[k, a], s_send.at[step, k, a], s_recv.at[step, k, a],
            peer_of(mod3(turn(k, a) + step)),
        )

    def give_send(step, k, a):
        size = (4, 2, 1)[step] * block
        return remote(
            delta.at[k, a, pl.ds(0, size)], delta.at[k, a, pl.ds(size, size)], g_send.at[step, k, a], g_recv.at[step, k, a],
            peer_of(mod3(back_turn(k, a) + step)),
        )

    def got_weight(k, a):
        own_weight(k, a).wait()
        sent_weight(k, a).wait_recv()

    def forward_in(first, count, wait=False):
        def step(k, carry):
            for a, buf in ((0, w_gate), (1, w_up)):
                if wait:
                    got_weight(k, a)
                rows = rows_in[0, first * block : (first + count) * block, :]
                value = jnp.dot(rows, buf[k], preferred_element_type=F32).astype(BF16)
                places = weights_of(turn(k, a))
                for j in range(count):
                    slot = slot_of(places, ORDER[first + j])
                    part[k, a, span(slot), :] = value[j * block : (j + 1) * block]

                    @pl.when(slot >= 4)
                    def _():
                        remote(
                            part.at[k, a, span(slot)], land1.at[k, a, span(slot - 4)],
                            s_send.at[0, k, a], s_recv.at[0, k, a], peer_of(turn(k, a)),
                        ).start()

            return carry

        return step

    def forward_out(k):
        got_weight(k, 2)
        value = lax.dot_general(rows_in[1], w_down[k], NT, preferred_element_type=F32).astype(BF16)
        places = weights_of(turn(k, 2))
        for j, name in enumerate(ORDER):
            part[k, 2, span(slot_of(places, name)), :] = value[j * block : (j + 1) * block]
        sum_send(0, k, 2).start()

    pass_on(0, 0, 3, 4)
    from_core(0, 7, 1, 2)
    lax.fori_loop(0, chunks, forward_in(0, 3, True), 0)
    pass_on(0, 3, 5)
    pass_on(0, 6)
    pass_on(0, 4)
    pass_on(1, 2, 6)
    pass_on(1, 1)
    pass_on(1, 0, 3, 4)
    start_weights(own_weight, (2,), 0, chunks)
    start_weights(sent_weight, (2,), 0, chunks)
    from_core(0, 0, 3, 4, 6)
    lax.fori_loop(0, chunks, forward_in(3, 4), 0)
    pass_on(0, 5)
    pass_on(1, 3, 5)
    pass_on(1, 6)
    pass_on(1, 4)
    from_core(0, 5)
    lax.fori_loop(0, chunks, forward_in(7, 1), 0)
    pass_on(1, 5)
    from_core(1, *range(8))
    def add_in(k, a, land, first, count):
        for b in range(first, first + count):
            at = pl.ds(b * block, block)
            part[k, a, at, :] = part[k, a, at, :] + land[k, a, at, :]

    def sum_stage(step, k, arrays=(0, 1, 2)):
        land = (land1, land2)[step]
        keep = (2, 1)[step]
        for a in arrays:
            sum_send(step, k, a).wait_recv()
            add_in(k, a, land, keep, keep)
            sum_send(step + 1, k, a).start()
            add_in(k, a, land, 0, keep)

    def activate(k):
        for a in range(3):
            sum_send(2, k, a).wait_recv()
        piece = 32

        def act_step(i, carry):
            at = pl.ds(pl.multiple_of(i * piece, piece), piece)
            gate, upper, back = (part[k, a, at, :].astype(F32) + land3[k, a, at, :].astype(F32) for a in range(3))
            sig = jax.nn.sigmoid(gate)
            silu = gate * sig
            delta[k, 0, at, :] = (back * upper * sig * (1.0 + gate * (1.0 - sig))).astype(BF16)
            delta[k, 1, at, :] = (back * silu).astype(BF16)
            delta[k, 2, at, :] = (silu * upper).astype(BF16)
            return carry

        lax.fori_loop(0, block // piece, act_step, 0)
        for a in range(3):
            give_send(2, k, a).start()

    def give_stage(step, k, arrays=(0, 1)):
        for a in arrays:
            give_send(step, k, a).wait_recv()
            give_send(step - 1, k, a).start()
            if a == 2:
                give_send(step, k, a).wait_send()

    outs = (out_g, out_u, out_h)

    def out_from(k, a, side):
        return staged_down.at[k, :, side_of(side)] if a == 2 else staged.at[k % 2, a, side_of(side), :]

    def own_out(k, a):
        return local(out_from(k, a, core), chunk_of(outs[a], core, k, a == 2), o_local.at[k, a])

    def core_out(k, a, side=core):
        return remote(
            out_from(k, a, mate), chunk_of(outs[a], side, k, a == 2), o_send.at[k, a], o_recv.at[k, a], peer_core
        )

    def finish(k, a):
        give_send(0, k, a).wait_recv()
        for step in range(3):
            sum_send(step, k, a).wait_send()
        places = weights_of(back_turn(k, a))
        for name in ORDER:
            part[k, a, held(name), :] = delta[k, a, span(slot_of(places, name)), :]
        if a == 2:
            give_send(0, k, a).wait_send()
            tokens = 8 * block
            for at in range(0, tokens, 128):
                hidden_turned[:, at : at + 128] = part[k, 2, at : at + 128, :].T
            value = jnp.dot(hidden_turned[...], rows_in[1], preferred_element_type=F32)
            staged_down[k] = (value * factor).astype(BF16)
            own_out(k, a).start()
            core_out(k, a).start()

    def backward(k):
        for a in range(2):
            finish(k, a)
        total[...] = (
            total[...]
            + lax.dot_general(part[k, 0], w_gate[k], NT, preferred_element_type=F32)
            + lax.dot_general(part[k, 1], w_up[k], NT, preferred_element_type=F32)
        )

    def gradients(k):
        for a in range(2):
            value = jnp.dot(turned[...], part[k, a], preferred_element_type=F32)
            staged[k % 2, a] = (value * factor).astype(BF16)
            own_out(k, a).start()
            core_out(k, a).start()

    def settle_out(k, a):
        own_out(k, a).wait()
        core_out(k, a).wait_send()
        core_out(k, a, mate).wait_recv()

    def settle(k):
        for a in range(2):
            for step in range(3):
                give_send(step, k, a).wait_send()
            settle_out(k, a)

    def settle_inputs():
        def step(k, carry):
            for a in range(3):
                sent_weight(k, a).wait_send()
            return carry

        lax.fori_loop(0, chunks, step, 0)
        for t in range(2):
            for m in range(7):
                gather_send(t, m).wait_send()
            for m in range(8):
                to_core(t, m).wait_send()

    def turn_inputs():
        for at in range(0, 2 * feats, 128):
            turned[at : at + 128, :] = rows_in[0, :, at : at + 128].T

    def late_give(first, last):
        def step(k, carry):
            give_stage(1, k, (2,))
            return carry

        lax.fori_loop(min(first, chunks), min(last, chunks), step, 0)

    ahead = min(3, chunks)

    def first_out(k, carry):
        forward_out(k)
        return carry

    def first_sums(k, carry):
        sum_stage(0, k, (0, 1))
        return carry

    lax.fori_loop(0, ahead, first_out, 0)
    lax.fori_loop(0, ahead, first_sums, 0)

    def slot_step(i, carry):
        @pl.when(i + ahead < chunks)
        def _():
            forward_out(i + ahead)
            sum_stage(0, i + ahead, (0, 1))

        def stage(lag, run):
            @pl.when(jnp.logical_and(i >= lag, i < chunks + lag))
            def _():
                run(i - lag)

        stage(0, lambda k: sum_stage(0, k, (2,)))
        stage(1, functools.partial(sum_stage, 1))
        stage(2, activate)
        stage(3, functools.partial(give_stage, 2))
        stage(4, functools.partial(give_stage, 1))
        stage(5, backward)
        stage(6, gradients)
        stage(7, settle)

        @pl.when(i == 2)
        def _():
            settle_inputs()

        @pl.when(i == 0)
        def _():
            turn_inputs()

        @pl.when(i >= chunks)
        def _():
            first = 2 * (i - chunks)
            for k in (first, first + 1):
                @pl.when(k < chunks)
                def _():
                    give_stage(2, k, (2,))

        @pl.when(i == chunks + 3)
        def _():
            late_give(0, 3)

        return carry

    lax.fori_loop(0, chunks + 5, slot_step, 0)

    def late_finish(first, last):
        def step(k, carry):
            finish(k, 2)
            return carry

        lax.fori_loop(min(first, chunks), min(last, chunks), step, 0)

    late_give(3, chunks)

    cored = ("far", "far_m", "up_m", "dn", "up", "dn_m", "mate", "own")

    def core_sum(n):
        at = held(cored[n])
        return remote(mate_send.at[at], mate_land.at[at], t_send.at[7 + n], t_recv.at[7 + n], peer_core)

    for n, name in enumerate(cored):
        mate_send[held(name), :] = total[held(name), side_of(mate)].astype(BF16)
        core_sum(n).start()

    def core_add(n):
        core_sum(n).wait_recv()
        at = held(cored[n])
        both = total[at, side_of(core)] + mate_land[at, :].astype(F32)
        if n < 4:
            side_send[at, :] = both.astype(BF16)
        else:
            total[at, side_of(core)] = both

    def mine(name):
        return total[held(name), side_of(core)]

    def send_block(m, name, peer):
        return remote(side_send.at[held(name)], side_land.at[m], t_send.at[m], t_recv.at[m], peer)

    far_up = send_block(0, "far", peer_up)
    far_dn = send_block(1, "far_m", peer_dn)
    one_up = send_block(2, "up_m", peer_up)
    one_dn = send_block(3, "dn", peer_dn)
    two_up = send_block(4, "up", peer_up)
    two_dn = send_block(5, "dn_m", peer_dn)
    core_add(0)
    far_up.start()
    core_add(1)
    far_dn.start()
    core_add(2)
    one_up.start()
    core_add(3)
    one_dn.start()
    for n in range(4, 8):
        core_add(n)
    gradients(chunks - 1)
    late_finish(0, 2)
    far_up.wait_recv()
    side_send[held("up"), :] = (mine("up") + side_land[0].astype(F32)).astype(BF16)
    two_up.start()
    far_dn.wait_recv()
    side_send[held("dn_m"), :] = (mine("dn_m") + side_land[1].astype(F32)).astype(BF16)
    two_dn.start()
    late_finish(2, 6)
    one_up.wait_recv()
    two_dn.wait_recv()
    side_send[held("mate"), :] = (mine("mate") + side_land[2].astype(F32) + side_land[5].astype(F32)).astype(BF16)
    one_dn.wait_recv()
    two_up.wait_recv()
    total[held("own"), side_of(core)] = mine("own") + side_land[3].astype(F32) + side_land[4].astype(F32)
    results = (
        local(side_send.at[held("mate")], mate_out, xo_sem.at[0]),
        local(total.at[held("own"), side_of(core)], kept_out, xo_sem.at[1]),
    )
    for copy in results:
        copy.start()
    late_finish(6, chunks)

    for k in range(max(chunks - 2, 0), chunks):
        settle(k)

    def settle_hidden(k, carry):
        settle_out(k, 2)
        return carry

    lax.fori_loop(0, chunks, settle_hidden, 0)
    for n in range(8):
        core_sum(n).wait_send()
    for copy in (far_up, far_dn, one_up, one_dn, two_up, two_dn):
        copy.wait_send()
    for copy in results:
        copy.wait()


def pass_kernel(gate_in, up_in, down_in, gate_grad, up_grad, down_grad):
    gate_grad[...] = gate_in[...]
    up_grad[...] = up_in[...]
    down_grad[...] = down_in[...]


def pass_through(*grads):
    steps = 2
    rows = [pl.BlockSpec((grad.shape[0] // steps, grad.shape[1]), lambda i: (i, 0)) for grad in grads]
    return pl.pallas_call(
        pass_kernel,
        grid=(steps,),
        out_shape=[jax.ShapeDtypeStruct(grad.shape, BF16) for grad in grads],
        in_specs=rows,
        out_specs=rows,
        compiler_params=pltpu.CompilerParams(vmem_limit_bytes=62 * 2**20),
        cost_estimate=pl.CostEstimate(
            flops=0, bytes_accessed=4 * sum(grad.size for grad in grads), transcendentals=0
        ),
        name="pass_kernel",
    )(*grads)


def per_device(acts, logits, label_ids, head_weight, gate_weight, up_weight, down_weight):
    tokens = acts.shape[0] * 8
    width, feats = gate_weight.shape[1], acts.shape[1]
    block = acts.shape[0]
    chunks = width // 2 // WIDE
    any_spec = pl.BlockSpec(memory_space=pl.ANY)
    dma = pltpu.SemaphoreType.DMA
    grads_shape = jax.ShapeDtypeStruct((feats, width), BF16)
    down_grad, gate_grad, up_grad, kept, passed = pl.pallas_call(
        functools.partial(layer_kernel, chunks, 1.0 / tokens**0.5),
        out_shape=(
            jax.ShapeDtypeStruct((width, feats), BF16), grads_shape, grads_shape,
            jax.ShapeDtypeStruct(acts.shape, F32), jax.ShapeDtypeStruct(acts.shape, BF16),
        ),
        in_specs=[any_spec] * 7,
        out_specs=(any_spec,) * 5,
        scratch_shapes=[
            pltpu.VMEM((2, tokens, 2 * feats), BF16),
            pltpu.VMEM((chunks, 2 * feats, WIDE), BF16),
            pltpu.VMEM((chunks, 2 * feats, WIDE), BF16),
            pltpu.VMEM((chunks, WIDE, 2 * feats), BF16),
            pltpu.VMEM((chunks, 3, tokens, WIDE), BF16),
            pltpu.VMEM((chunks, 3, 4 * block, WIDE), BF16),
            pltpu.VMEM((chunks, 3, 2 * block, WIDE), BF16),
            pltpu.VMEM((chunks, 3, block, WIDE), BF16),
            pltpu.VMEM((chunks, 3, tokens, WIDE), BF16),
            pltpu.VMEM((tokens, 2 * feats), F32),
            pltpu.VMEM(logits.shape, F32),
            pltpu.VMEM(label_ids.shape[::-1], jnp.int32),
            pltpu.VMEM(label_ids.shape, jnp.int32),
            pltpu.VMEM(head_weight.shape, BF16),
            pltpu.VMEM(logits.shape, BF16),
            pltpu.VMEM((2 * feats, tokens), BF16),
            pltpu.VMEM((WIDE, tokens), BF16),
            pltpu.VMEM((2, 2, 2 * feats, WIDE), BF16),
            pltpu.VMEM((chunks, WIDE, 2 * feats), BF16),
            pltpu.VMEM((tokens, feats), BF16),
            pltpu.VMEM((tokens, feats), BF16),
            pltpu.VMEM((tokens, feats), BF16),
            pltpu.VMEM((6, block, feats), BF16),
            dma((4,)), dma((chunks, 3)), dma((chunks, 3)), dma((chunks, 3)),
            dma((2, 7)), dma((2, 7)), dma((2, 8)), dma((2, 8)),
            dma((3, chunks, 3)), dma((3, chunks, 3)), dma((3, chunks, 3)), dma((3, chunks, 3)),
            dma((chunks, 3)), dma((chunks, 3)), dma((chunks, 3)), dma((15,)), dma((15,)), dma((2,)),
        ],
        compiler_params=pltpu.CompilerParams(collective_id=0, has_side_effects=True, vmem_limit_bytes=60 * 2**20),
        name="layer_kernel",
    )(acts, logits, label_ids.T, head_weight, gate_weight, up_weight, down_weight)
    swapped = lax.ppermute(passed, "row", [(at, at + 1 - 2 * (at % 2)) for at in range(8)])
    acts_grad = (kept + swapped.astype(F32)).astype(BF16)
    gate_grad, up_grad, down_grad = pass_through(gate_grad, up_grad, down_grad)
    return acts_grad, gate_grad, up_grad, down_grad


def solution(mesh):
    placed = (
        P("row", "col"),
        P("row", None),
        P("row", None),
        P(None, "col"),
        P("col", "row"),
        P("col", "row"),
        P("row", "col"),
    )
    return jax.shard_map(
        per_device,
        mesh=mesh,
        in_specs=placed,
        out_specs=(P("row", "col"), P("col", "row"), P("col", "row"), P("row", "col")),
        check_vma=False,
    )
```
